256 devices in a mesh: seq: 8 (over z), exp: 32 (over x, y, core).
Axes of the slice: x: 4, y: 4, z: 8, core: 2. Of those that a mesh axis runs over, the one named last changes fastest.
Arguments:
- tokens: bfloat16 [32, 512, 4096], P('exp', 'seq'), may hold values from -6 to 6
- queries: bfloat16 [32, 512, 4096], P('exp', 'seq'), may hold values from -6 to 6
- memory_kv: bfloat16 [512, 1024], P('exp'), may hold values from -6 to 6
- memory_pos: int32 [512], P('exp'), may hold values from 0 to 1023
- out_weight: bfloat16 [4096, 4096], P('seq'), may hold values from -1.5 to 1.5
- norm_gain: float32 [4096], replicated, may hold values from 0.5 to 1.5
- routes: int32 [32, 512, 2], P('exp', 'seq'), may hold values from 0 to 31, all different within a row; in each aligned block of 64 rows (0 to 63, 64 to 127, ..., all dimensions but the last counted through in order) at most 5 rows name the same one
- route_weights: float32 [32, 512, 2], P('exp', 'seq'), may hold values from 0.05 to 1
- gate_w: bfloat16 [32, 4096, 1536], P('exp', None, 'seq'), may hold values from -0.09375 to 0.09375
- up_w: bfloat16 [32, 4096, 1536], P('exp', None, 'seq'), may hold values from -0.09375 to 0.09375
- down_w: bfloat16 [32, 1536, 4096], P('exp', 'seq'), may hold values from -0.15625 to 0.15625
Outputs:
- attended: bfloat16 [32, 512, 4096], P('exp', 'seq')
- mixture: bfloat16 [32, 512, 4096], P('exp', 'seq')
The draws below stay inside these ranges and needn't reach their ends.
Inputs may be any that keep to these rules, and one draw needn't show every extreme that they name: `routes`: each token names 2 different experts. Taking the tokens in order of span and then place, among each aligned block of 64 tokens (the tokens of one device) no expert is named more than 5 times, and in every draw some expert is named exactly 5 times within one block.
All inputs are finite; a program needn't handle non-finite values.
Results may differ from the reference program's by a relative error of at most 0.035.
Values may be sent and summed in bfloat16 or wider, within the bound.
A program may use at most 128 MiB of HBM per device.

```python
import math
import jax
import jax.numpy as jnp
import numpy as np
from jax import lax

D = 4096
HQ = 32
KVH = 4
HD = 128
FF = 1536
EXPERTS = 32
TOPK = 2
TOK_DEV = 64
CAP = 5
SPAN = 512
SEQS = 32
MEM = 512
N_SEQ = 8
N_EXP = 32


def touch_ends(values, stream_key, smallest, high):
    extent = values.shape
    place = [jax.random.randint(jax.random.fold_in(stream_key, axis), (), 0, extent[axis]) for axis in range(len(extent))]
    values = values.at[tuple(place)].set(smallest)
    longest = extent.index(max(extent))
    place[longest] = (place[longest] + 1) % extent[longest]
    return values.at[tuple(place)].set(high)


def block_levels(stream_key, dims, cuts, smallest, high):
    loudness, own = 1.0, jax.random.fold_in(stream_key, 6)
    for position, shards_of in cuts:
        draws = jnp.exp(jax.random.uniform(jax.random.fold_in(own, position), (shards_of,), jnp.float32, smallest / len(cuts), high / len(cuts)))
        loudness = loudness * jnp.repeat(draws, dims[position] // shards_of).reshape([-1 if axis == position else 1 for axis in range(len(dims))])
    return loudness


def assign_block(stream_key, own, number, rows, number_of, top, most, lean):
    sequence = jax.random.permutation(stream_key, number_of)
    packed, ordinary = load_shares(number_of, rows * top, most, lean, True), load_shares(number_of, rows * top, most, lean, False)
    places = jnp.arange(number_of)

    def named(lengths, rotation):
        used = int((lengths > 0).sum())
        fixed = max(1, used // 4)
        shifted = fixed + (places - fixed + rotation * (used - fixed)) % max(1, number_of - fixed)
        return jnp.zeros((number_of,), jnp.int32).at[sequence[jnp.where(places < fixed, places, shifted)]].set(jnp.asarray(lengths, jnp.int32))

    lengths = jnp.where(number % 4 == 0, named(packed, number // 4), named(ordinary, number - number // 4 - 1))
    mixed = jax.random.permutation(jax.random.fold_in(own, 3), number_of)
    giver, taker = mixed[0:number_of // 2 * 2:2], mixed[1:number_of // 2 * 2:2]
    margin = jnp.minimum(lengths[giver] - 1, most - lengths[taker]) // 2
    margin = jnp.where((giver == sequence[0]) | (taker == sequence[0]) | (lengths[taker] == 0), 0, jnp.maximum(margin, 0))
    shifted = jax.random.randint(jax.random.fold_in(own, 4), (number_of // 2,), 0, 1 << 20) % (margin + 1)
    lengths = lengths.at[giver].add(-shifted).at[taker].add(shifted)
    items = jnp.searchsorted(jnp.cumsum(lengths), jnp.arange(rows * top), side="right").astype(jnp.int32)
    table = items.reshape(top, rows).T
    table = table[jax.random.permutation(jax.random.fold_in(own, 1), rows)]
    rotation = jax.random.randint(jax.random.fold_in(own, 2), (rows, 1), 0, top)
    return jnp.take_along_axis(table, (jnp.arange(top)[None, :] + rotation) % top, axis=1)


def load_shares(number_of, total, reach, skew, full):
    portions = [(1 << 20) // math.isqrt(standing ** skew) + 1 for standing in range(1, number_of + 1)]
    largest = reach if full else min(reach, max(-(-total // number_of), total * portions[0] // sum(portions)))
    least = 1 if total - largest >= number_of - 1 else 0
    holding, surplus = [largest] + [least] * (number_of - 1), total - largest - least * (number_of - 1)
    while surplus > 0:
        movable = [i for i in range(1, number_of) if holding[i] < largest] or [i for i in range(1, number_of) if holding[i] < reach]
        whole, remaining = sum([portions[i] for i in movable]), surplus
        for i in movable:
            more = min(reach - holding[i], max(1, remaining * portions[i] // whole), surplus)
            holding[i] = holding[i] + more
            surplus = surplus - more
    return np.array(holding)


def gaussian(own_key, dims, width, reach, pieces=(), kind=jnp.bfloat16):
    values = jax.random.normal(own_key, dims, jnp.float32) * width
    if len(pieces) > 0:
        values = block_levels(own_key, dims, pieces, -0.22, 0.18) * values
    return jnp.clip(values, min=-reach, max=reach).astype(kind)


def setup_inputs(seed: int = 0) -> dict:
    key_of = jax.random.split(jax.random.key(seed), 12)
    tokens = gaussian(key_of[0], (SEQS, SPAN, D), 1.0, 6.0, ((0, 32), (1, 8)))
    queries = gaussian(key_of[1], (SEQS, SPAN, HQ * HD), 1.0, 6.0, ((0, 32), (1, 8)))
    memory_kv = gaussian(key_of[2], (MEM, KVH * 2 * HD), 1.0, 6.0, ((0, 32),))
    memory_pos = touch_ends(jax.random.randint(key_of[3], (MEM,), 0, 2 * SPAN), jax.random.fold_in(key_of[3], 1), 0, (2 * SPAN) - 1).astype(jnp.int32)
    out_weight = gaussian(key_of[4], (HQ * HD, D), 0.25, 1.5, ((0, 8),))
    norm_gain = jnp.clip(1.0 + 0.1 * jax.random.normal(key_of[5], (D,), jnp.float32), 0.5, 1.5)
    routes_keys = jax.random.split(jax.random.fold_in(key_of[6], 1), SEQS * SPAN // TOK_DEV)
    routes_turns = jax.random.permutation(jax.random.fold_in(key_of[6], 3), SEQS * SPAN // TOK_DEV)
    routes = jax.vmap(lambda own, number: assign_block(jax.random.fold_in(key_of[6], 2), own, number, TOK_DEV, EXPERTS, TOPK, CAP, 2))(routes_keys, routes_turns).reshape((SEQS, SPAN, TOPK))
    route_weights = jnp.clip(jnp.exp(math.log(1.0) - 2.9957323 * jax.random.uniform(key_of[7], (SEQS, SPAN, TOPK), jnp.float32) ** block_levels(key_of[7], (SEQS, SPAN, TOPK), ((0, 32), (1, 8)), -0.2, 0.2)), 0.05, 1.0)
    gate_w = gaussian(key_of[8], (EXPERTS, D, FF), D ** -0.5, 0.09375, ((0, 32), (2, 8)))
    up_w = gaussian(key_of[9], (EXPERTS, D, FF), D ** -0.5, 0.09375, ((0, 32), (2, 8)))
    down_w = gaussian(key_of[10], (EXPERTS, FF, D), FF ** -0.5, 0.15625, ((0, 32), (1, 8)))
    return dict(tokens=tokens, queries=queries, memory_kv=memory_kv, memory_pos=memory_pos, out_weight=out_weight, norm_gain=norm_gain, routes=routes, route_weights=route_weights, gate_w=gate_w, up_w=up_w, down_w=down_w)


def reference(tokens, queries, memory_kv, memory_pos, out_weight, norm_gain, routes, route_weights, gate_w, up_w, down_w):
    total_tokens = SEQS * SPAN
    group_size = HQ // KVH
    score_scale = 1.0 / math.sqrt(HD)
    flat_queries = queries.reshape(total_tokens, HQ * HD)
    flat_tokens = tokens.reshape(total_tokens, D)
    query_pos = SPAN + jnp.arange(total_tokens, dtype=jnp.int32) % SPAN
    visible = memory_pos[None, :] <= query_pos[:, None]

    def one_head(head_index):
        query_cols = lax.dynamic_slice_in_dim(flat_queries, head_index * HD, HD, 1)
        kv_start = head_index // group_size * (2 * HD)
        key_rows = lax.dynamic_slice_in_dim(memory_kv, kv_start, HD, 1)
        value_rows = lax.dynamic_slice_in_dim(memory_kv, kv_start + HD, HD, 1)
        scores = jnp.dot(query_cols, key_rows.T, preferred_element_type=jnp.float32) * score_scale
        scores = jnp.where(visible, scores, -1e+30)
        top_score = lax.optimization_barrier(jnp.max(scores, axis=1, keepdims=True))
        weights = jnp.exp(scores - top_score)
        probabilities = (weights / lax.optimization_barrier(jnp.sum(weights, axis=1, keepdims=True))).astype(jnp.bfloat16)
        return jnp.dot(probabilities, value_rows, preferred_element_type=jnp.float32).astype(jnp.bfloat16)
    context = lax.map(one_head, jnp.arange(HQ, dtype=jnp.int32))
    context = jnp.transpose(context, (1, 0, 2)).reshape(total_tokens, HQ * HD)
    head_share = HQ * HD // N_SEQ
    head_parts = jnp.einsum('tsc,scd->std', context.reshape(total_tokens, N_SEQ, head_share).astype(jnp.float32), out_weight.reshape(N_SEQ, head_share, D).astype(jnp.float32), precision=lax.Precision.HIGHEST)
    head_rounded = lax.optimization_barrier(head_parts.astype(jnp.bfloat16))
    projected = lax.optimization_barrier(jnp.sum(head_rounded.astype(jnp.float32), axis=0))
    attended = projected.astype(jnp.bfloat16)
    summed = flat_tokens.astype(jnp.float32) + projected
    normed = (summed * lax.rsqrt(lax.optimization_barrier(jnp.mean(summed * summed, axis=1, keepdims=True)) + 1e-06) * norm_gain).astype(jnp.bfloat16)
    flat_routes = routes.reshape(-1)
    row_total = total_tokens * TOPK
    flat_order = jnp.arange(row_total, dtype=jnp.int32)
    token_index = flat_order // TOPK
    flat_weights = route_weights.reshape(-1)
    slot_count = N_SEQ * N_EXP * CAP
    unit_share = FF // N_SEQ

    def one_expert(running, expert):
        key_order = jnp.where(flat_routes == expert, flat_order, row_total)
        picked = jnp.sort(key_order)[:slot_count]
        is_valid = picked < row_total
        chosen = jnp.minimum(picked, row_total - 1)
        target = token_index[chosen]
        inputs = normed[target]
        gate_act = jnp.dot(inputs, gate_w[expert], preferred_element_type=jnp.float32)
        up_act = jnp.dot(inputs, up_w[expert], preferred_element_type=jnp.float32)
        hidden = (jax.nn.silu(gate_act) * up_act).astype(jnp.bfloat16)
        partials = jnp.einsum('rsf,sfd->srd', hidden.reshape(slot_count, N_SEQ, unit_share).astype(jnp.float32), down_w[expert].reshape(N_SEQ, unit_share, D).astype(jnp.float32), precision=lax.Precision.HIGHEST)
        rounded = lax.optimization_barrier(partials.astype(jnp.bfloat16))
        output = lax.optimization_barrier(jnp.sum(rounded.astype(jnp.float32), axis=0)).astype(jnp.bfloat16)
        scaled = output.astype(jnp.float32) * jnp.where(is_valid, flat_weights[chosen], 0.0)[:, None]
        return (running.at[target].add(scaled), None)
    mixture, unused = lax.scan(one_expert, jnp.zeros((total_tokens, D), jnp.float32), jnp.arange(EXPERTS, dtype=jnp.int32))
    return (attended.reshape(SEQS, SPAN, D), mixture.astype(jnp.bfloat16).reshape(SEQS, SPAN, D))
```

```python
import functools
import math

import jax
import jax.numpy as jnp
from jax import lax
from jax.experimental import pallas as pl
from jax.experimental.pallas import tpu as pltpu
from jax.sharding import PartitionSpec as P

MESH = pl.DeviceIdType.MESH
EXPERTS = 32
CAP = 5
RING = 8
D = 4096
HALF = D // 2
HD = 128
TOK = 64
MEM = 512
KEYS = 512
UNITS = 192
SLOTS = EXPERTS * CAP
LANES = HALF // 128
PIECE = LANES * CAP
F32 = jnp.float32
BF16 = jnp.bfloat16

HOPS = [
    (dx, dy, dc)
    for dc in range(2)
    for dx, dy in [
        (2, 2), (1, 1), (3, 3), (2, 1), (1, 2), (2, 3), (3, 2), (1, 3),
        (3, 1), (2, 0), (0, 2), (1, 0), (3, 0), (0, 1), (0, 3), (0, 0),
    ]
    if (dx, dy, dc) != (0, 0, 0)
]


def exp_peers(e):
    x, y, c = e // 8, (e // 2) % 4, e % 2
    return [((x + dx) % 4 * 8) + ((y + dy) % 4 * 2) + (c + dc) % 2 for dx, dy, dc in HOPS]


def cols(half):
    return pl.ds(half * HALF, HALF)


def ring_send(src, dst, sems, way, step, half, z, e):
    target = ((z + (1 if way == 0 else RING - 1)) % RING, e)
    copy = pltpu.make_async_remote_copy(
        src_ref=src,
        dst_ref=dst,
        send_sem=sems[0].at[way, step, half],
        recv_sem=sems[1].at[way, step, half],
        device_id=target,
        device_id_type=MESH,
    )
    copy.start()
    return copy


def reduce_ring(stage, land, sems, z, e, sent, compute, early):
    def push(way, step, half):
        k = (4 - step) if way == 0 else (4 + step) % RING
        sent[way, step, half] = ring_send(
            stage.at[k, :, cols(half)], land.at[way, step, :, cols(half)], sems, way, step, half, z, e
        )

    def add(way, step, half):
        k = (4 - step) if way == 0 else (4 + step) % RING
        sent[way, step - 1, half].wait_recv()
        stage[k, :, cols(half)] = (
            stage[k, :, cols(half)].astype(F32) + land[way, step - 1, :, cols(half)].astype(F32)
        ).astype(BF16)

    if early:
        push(0, 1, 0)
        push(1, 1, 1)
    compute(4)
    push(1, 0, 0)
    push(0, 0, 1)
    if not early:
        compute(3)
        push(0, 1, 0)
        compute(5)
        push(1, 1, 1)
    add(0, 1, 1)
    push(0, 1, 1)
    add(1, 1, 0)
    push(1, 1, 0)
    for step in (2, 3):
        if not early:
            compute(4 - step)
            compute(4 + step)
        for halves in ((0, 1), (1, 0)):
            for way in (0, 1):
                add(way, step, halves[way])
                push(way, step, halves[way])
    if not early:
        compute(0)


def attention_kernel(
    tokens, queries, memory, places, out_weight, gain,
    attended, normed,
    weight, qbuf, kvbuf, posbuf, stage, land, total,
    wsem, lsem, qs, qr, ks, kr, ps, pr, rs, rr,
):
    z, e = lax.axis_index("seq"), lax.axis_index("exp")
    load = pltpu.make_async_copy(out_weight, weight, wsem)
    load.start()
    barrier = pltpu.get_barrier_semaphore()
    peers = exp_peers(e)
    for k in range(1, RING):
        pl.semaphore_signal(barrier, inc=1, device_id=((z + k) % RING, e), device_id_type=MESH)
    for p in peers:
        pl.semaphore_signal(barrier, inc=1, device_id=(z, p), device_id_type=MESH)
    pair = pl.multiple_of(z // 2 * 256, 256)
    local = [
        pltpu.make_async_copy(queries.at[:, pl.ds(pl.multiple_of(z * KEYS, KEYS), KEYS)], qbuf.at[0], lsem.at[0]),
        pltpu.make_async_copy(memory.at[:, pl.ds(pair, 256)], kvbuf.at[31], lsem.at[1]),
        pltpu.make_async_copy(places, posbuf.at[31], lsem.at[2]),
    ]
    for c in local:
        c.start()
    pl.semaphore_wait(barrier, RING - 1 + len(peers))
    queue = {}
    for k in (4, 3, 5, 2, 6, 1, 7):
        to = (z + k) % RING
        queue[RING - k] = pltpu.make_async_remote_copy(
            src_ref=queries.at[:, pl.ds(pl.multiple_of(to * KEYS, KEYS), KEYS)],
            dst_ref=qbuf.at[RING - k],
            send_sem=qs.at[k],
            recv_sem=qr.at[RING - k],
            device_id=(to, e),
            device_id_type=MESH,
        )
        queue[RING - k].start()
    moved = []
    for n, p in enumerate(peers):
        for src, dst, s, r in ((memory.at[:, pl.ds(pair, 256)], kvbuf, ks, kr), (places, posbuf, ps, pr)):
            c = pltpu.make_async_remote_copy(
                src_ref=src, dst_ref=dst.at[n], send_sem=s.at[n], recv_sem=r.at[n],
                device_id=(z, p), device_id_type=MESH,
            )
            c.start()
            moved.append(c)
    for c in local:
        c.wait()
    for c in moved:
        c.wait()
    load.wait()

    def compute(k):
        if k:
            queue[k].wait_recv()
        block = qbuf[k]
        stacked = jnp.concatenate([block[:, h * HD:(h + 1) * HD] for h in range(4)], axis=0)
        key_rows = kvbuf[:, :, 0:HD].reshape(MEM, HD)
        value_rows = kvbuf[:, :, HD:2 * HD].reshape(MEM, HD)
        scores = lax.dot_general(
            key_rows, stacked, (((1,), (1,)), ((), ())), preferred_element_type=F32
        ) * (1.0 / math.sqrt(HD))
        limit = MEM + (z + k) % RING * TOK + lax.broadcasted_iota(jnp.int32, (1, 4 * TOK), 1) % TOK
        where = posbuf[...].reshape(MEM, 128)
        where = jnp.concatenate([where, where], axis=1)
        scores = jnp.where(where <= limit, scores, -1e30)
        top = jnp.max(scores, axis=0, keepdims=True)
        weights = jnp.exp(scores - top)
        probs = (weights / jnp.sum(weights, axis=0, keepdims=True)).astype(BF16)
        context = lax.dot_general(
            probs, value_rows, (((0,), (0,)), ((), ())), preferred_element_type=F32
        ).astype(BF16)
        context = jnp.concatenate([context[h * TOK:(h + 1) * TOK] for h in range(4)], axis=1)

        @pl.loop(0, 4)
        def _(c):
            part = pl.ds(pl.multiple_of(c * 1024, 1024), 1024)
            stage[k, :, part] = jnp.dot(
                context, weight[:, part], preferred_element_type=F32
            ).astype(BF16)

    sent = {}
    reduce_ring(stage, land, (rs, rr), z, e, sent, compute, False)
    square = jnp.zeros((TOK, 1), F32)
    for half in range(2):
        sent[0, 3, half].wait_recv()
        sent[1, 3, half].wait_recv()
        projected = (
            stage[0, :, cols(half)].astype(F32)
            + land[0, 3, :, cols(half)].astype(F32)
            + land[1, 3, :, cols(half)].astype(F32)
        )
        attended[:, cols(half)] = projected.astype(BF16)
        summed = tokens[:, cols(half)].astype(F32) + projected
        total[:, cols(half)] = summed
        square = square + jnp.sum(summed * summed, axis=1, keepdims=True)
    scale = lax.rsqrt(square * (1.0 / D) + 1e-6)
    for half in range(2):
        normed[:, cols(half)] = (total[:, cols(half)] * scale * gain[:, cols(half)]).astype(BF16)
    for c in queue.values():
        c.wait_send()
    for c in sent.values():
        c.wait_send()


def pack(rows, wide, out):
    for c in range(LANES):
        for r in range(CAP):
            wide[pl.ds(c * CAP + r, EXPERTS, stride=PIECE), :] = rows[
                r * EXPERTS:(r + 1) * EXPERTS, c * 128:(c + 1) * 128
            ]
    out[...] = wide[...].astype(BF16)


def unpack(got, wide, out, half):
    wide[...] = got[...].astype(F32)
    for c in range(LANES):
        for r in range(CAP):
            out[r * EXPERTS:(r + 1) * EXPERTS, half * HALF + c * 128:half * HALF + (c + 1) * 128] = wide[
                pl.ds(c * CAP + r, EXPERTS, stride=PIECE), :
            ].astype(BF16)


def expert_kernel(
    normed, pick, mixer, gate, up, down,
    mixture,
    gate_up, low, xs, stage, land, outgo, income, back, home, wide, returned,
    wsem, lsem, as_, ar, bs, br, gs, gr, rs, rr,
):
    z, e = lax.axis_index("seq"), lax.axis_index("exp")
    loads = [
        pltpu.make_async_copy(gate, gate_up.at[0:UNITS], wsem.at[0]),
        pltpu.make_async_copy(up, gate_up.at[UNITS:2 * UNITS], wsem.at[1]),
        pltpu.make_async_copy(down, low, wsem.at[2]),
    ]
    for c in loads:
        c.start()
    barrier = pltpu.get_barrier_semaphore()
    peers = exp_peers(e)
    for k in (1, RING - 1):
        pl.semaphore_signal(barrier, inc=1, device_id=((z + k) % RING, e), device_id_type=MESH)
    for p in peers:
        pl.semaphore_signal(barrier, inc=1, device_id=(z, p), device_id_type=MESH)

    def exchange(src, dst, half, send, recv):
        mine = pl.ds(pl.multiple_of(e * PIECE, 16), PIECE)
        copies = []
        for n, p in enumerate(peers):
            c = pltpu.make_async_remote_copy(
                src_ref=src.at[half, pl.ds(pl.multiple_of(p * PIECE, 16), PIECE)],
                dst_ref=dst.at[half, mine],
                send_sem=send.at[half, n],
                recv_sem=recv.at[half, n],
                device_id=(z, p),
                device_id_type=MESH,
            )
            c.start()
            copies.append(c)
        own = pltpu.make_async_copy(src.at[half, mine], dst.at[half, mine], send.at[half, 31])
        own.start()
        return copies, own

    def picked(half):
        return jnp.dot(pick[...], normed[:, cols(half)], preferred_element_type=F32)

    there, away = {}, {}
    pack(picked(0), wide, outgo.at[0])
    pl.semaphore_wait(barrier, 2 + len(peers))
    there[0] = exchange(outgo, income, 0, as_, ar)
    pack(picked(1), wide, outgo.at[1])
    there[1] = exchange(outgo, income, 1, as_, ar)

    gathered = {}

    def pass_on(way, step, half):
        k = (RING - step) % RING if way == 0 else step
        to = (k + RING - 1) % RING if way == 0 else k + 1
        gathered[way, step, half] = ring_send(
            xs.at[k, :, cols(half)], xs.at[to, :, cols(half)], (gs, gr), way, step, half, z, e
        )

    for half in range(2):
        copies, own = there[half]
        own.wait()
        for c in copies:
            c.wait_recv()
        unpack(income.at[half], wide, xs.at[0], half)
        pass_on(0, 0, half)
        pass_on(1, 0, half)
    for c in loads:
        c.wait()

    def compute(k):
        act = lax.dot_general(
            xs[k], gate_up[...], (((1,), (1,)), ((), ())), preferred_element_type=F32
        )
        gate_act, up_act = act[:, 0:UNITS], act[:, UNITS:2 * UNITS]
        hidden = (gate_act / (1.0 + jnp.exp(-gate_act)) * up_act).astype(BF16)

        @pl.loop(0, 4)
        def _(c):
            part = pl.ds(pl.multiple_of(c * 1024, 1024), 1024)
            stage[k, :, part] = jnp.dot(hidden, low[:, part], preferred_element_type=F32).astype(BF16)

    compute(0)
    for step in (1, 2):
        for half in range(2):
            for way in (0, 1):
                gathered[way, step - 1, half].wait_recv()
                pass_on(way, step, half)
        compute(step)
        compute(RING - step)
    gathered[0, 2, 0].wait_recv()
    pass_on(0, 3, 0)
    gathered[1, 2, 1].wait_recv()
    pass_on(1, 3, 1)
    gathered[0, 2, 1].wait_recv()
    gathered[1, 2, 0].wait_recv()
    compute(3)
    compute(5)

    def last(k):
        gathered[0, 3, 0].wait_recv()
        gathered[1, 3, 1].wait_recv()
        compute(k)

    sent = {}
    reduce_ring(stage, land, (rs, rr), z, e, sent, last, True)
    for half in range(2):
        sent[0, 3, half].wait_recv()
        sent[1, 3, half].wait_recv()
        rows = (
            stage[0, :, cols(half)].astype(F32)
            + land[0, 3, :, cols(half)].astype(F32)
            + land[1, 3, :, cols(half)].astype(F32)
        )
        pack(rows, wide, back.at[half])
        away[half] = exchange(back, home, half, bs, br)
    for half in range(2):
        copies, own = away[half]
        own.wait()
        for c in copies:
            c.wait_recv()
        unpack(home.at[half], wide, returned, half)
        both = jnp.dot(mixer[...], returned[:, cols(half)], preferred_element_type=F32)
        mixture[:, cols(half)] = (both[0:TOK] + both[TOK:2 * TOK]).astype(BF16)
    for half in range(2):
        for c in there[half][0] + away[half][0]:
            c.wait_send()
    for c in list(gathered.values()) + list(sent.values()):
        c.wait_send()


VM = pl.BlockSpec(memory_space=pltpu.VMEM)
HB = pl.BlockSpec(memory_space=pl.ANY)
DMA = pltpu.SemaphoreType.DMA


def body(tokens, queries, memory_kv, memory_pos, out_weight, norm_gain, routes, route_weights, gate_w, up_w, down_w):
    places = jnp.broadcast_to(memory_pos[:, None], (16, 128))
    attended, normed = pl.pallas_call(
        attention_kernel,
        name="attention",
        out_shape=[jax.ShapeDtypeStruct((TOK, D), BF16)] * 2,
        in_specs=[VM, VM, VM, VM, HB, VM],
        out_specs=[VM, VM],
        scratch_shapes=[
            pltpu.VMEM((KEYS, D), BF16),
            pltpu.VMEM((RING, TOK, KEYS), BF16),
            pltpu.VMEM((32, 16, 256), BF16),
            pltpu.VMEM((32, 16, 128), jnp.int32),
            pltpu.VMEM((RING, TOK, D), BF16),
            pltpu.VMEM((2, 4, TOK, D), BF16),
            pltpu.VMEM((TOK, D), F32),
            DMA, DMA((3,)), DMA((RING,)), DMA((RING,)),
            DMA((31,)), DMA((31,)), DMA((31,)), DMA((31,)),
            DMA((2, 4, 2)), DMA((2, 4, 2)),
        ],
        compiler_params=pltpu.CompilerParams(
            collective_id=0, has_side_effects=True, vmem_limit_bytes=40 * 2**20
        ),
    )(
        tokens.reshape(TOK, D), queries.reshape(TOK, D), memory_kv, places, out_weight,
        norm_gain.reshape(1, D),
    )

    names = routes.reshape(TOK, 2)
    one, two = names[:, 0], names[:, 1]
    before = jnp.arange(TOK)[:, None] > jnp.arange(TOK)[None, :]
    rank_one = jnp.sum((one[:, None] == one[None, :]) & before, axis=1, dtype=jnp.int32)
    rank_two = jnp.sum(two[:, None] == one[None, :], axis=1, dtype=jnp.int32) + jnp.sum(
        (two[:, None] == two[None, :]) & before, axis=1, dtype=jnp.int32
    )
    slot_one, slot_two = rank_one * EXPERTS + one, rank_two * EXPERTS + two
    ids = jnp.arange(SLOTS, dtype=jnp.int32)
    pick = ((slot_one[None, :] == ids[:, None]) | (slot_two[None, :] == ids[:, None])).astype(BF16)
    shares = route_weights.reshape(TOK, 2)
    mixer = jnp.where(slot_one[:, None] == ids[None, :], shares[:, 0:1], 0.0) + jnp.where(
        slot_two[:, None] == ids[None, :], shares[:, 1:2], 0.0
    )
    high = mixer.astype(BF16)
    mixer = jnp.concatenate([high, (mixer - high.astype(F32)).astype(BF16)], axis=0)

    mixture = pl.pallas_call(
        expert_kernel,
        name="experts",
        out_shape=jax.ShapeDtypeStruct((TOK, D), BF16),
        in_specs=[VM, VM, VM, HB, HB, HB],
        out_specs=VM,
        scratch_shapes=[
            pltpu.VMEM((2 * UNITS, D), BF16),
            pltpu.VMEM((UNITS, D), BF16),
            pltpu.VMEM((RING, SLOTS, D), BF16),
            pltpu.VMEM((RING, SLOTS, D), BF16),
            pltpu.VMEM((2, 4, SLOTS, D), BF16),
            pltpu.VMEM((2, EXPERTS * PIECE, 128), BF16),
            pltpu.VMEM((2, EXPERTS * PIECE, 128), BF16),
            pltpu.VMEM((2, EXPERTS * PIECE, 128), BF16),
            pltpu.VMEM((2, EXPERTS * PIECE, 128), BF16),
            pltpu.VMEM((EXPERTS * PIECE, 128), F32),
            pltpu.VMEM((SLOTS, D), BF16),
            DMA((3,)), DMA((1,)),
            DMA((2, 32)), DMA((2, 32)), DMA((2, 32)), DMA((2, 32)),
            DMA((2, 4, 2)), DMA((2, 4, 2)), DMA((2, 4, 2)), DMA((2, 4, 2)),
        ],
        compiler_params=pltpu.CompilerParams(
            collective_id=1, has_side_effects=True, vmem_limit_bytes=58 * 2**20
        ),
    )(
        normed, pick, mixer,
        jnp.swapaxes(gate_w[0], 0, 1), jnp.swapaxes(up_w[0], 0, 1), down_w[0],
    )
    return attended.reshape(1, TOK, D), mixture.reshape(1, TOK, D)


def solution(mesh):
    in_specs = (
        P("exp", "seq", None),
        P("exp", "seq", None),
        P("exp", None),
        P("exp"),
        P("seq", None),
        P(),
        P("exp", "seq", None),
        P("exp", "seq", None),
        P("exp", None, "seq"),
        P("exp", None, "seq"),
        P("exp", "seq", None),
    )
    out_specs = (P("exp", "seq", None), P("exp", "seq", None))
    return jax.shard_map(body, mesh=mesh, in_specs=in_specs, out_specs=out_specs, check_vma=False)
```

```python
import math

import jax
import jax.numpy as jnp
from jax import lax
from jax.experimental import pallas as pl
from jax.experimental.pallas import tpu as pltpu
from jax.sharding import PartitionSpec as P

MESH = pl.DeviceIdType.MESH
EXPERTS = 32
CAP = 5
RING = 8
D = 4096
WA = 2560
WB = D - WA
HA, HB2 = WA // 2, WB // 2
HD = 128
TOK = 64
MEM = 512
KEYS = 512
UNITS = 192
SLOTS = EXPERTS * CAP
PIECE = 64
F32 = jnp.float32
BF16 = jnp.bfloat16

HOPS = [
    (dx, dy, dc)
    for dc in range(2)
    for dx, dy in [
        (2, 2), (1, 1), (3, 3), (2, 1), (1, 2), (2, 3), (3, 2), (1, 3),
        (3, 1), (2, 0), (0, 2), (1, 0), (3, 0), (0, 1), (0, 3), (0, 0),
    ]
    if (dx, dy, dc) != (0, 0, 0)
]


def exp_peers(e):
    x, y, c = e // 8, (e // 2) % 4, e % 2
    return [((x + dx) % 4 * 8) + ((y + dy) % 4 * 2) + (c + dc) % 2 for dx, dy, dc in HOPS]


def ring_send(src, dst, send, recv, way, z, e):
    copy = pltpu.make_async_remote_copy(
        src_ref=src,
        dst_ref=dst,
        send_sem=send,
        recv_sem=recv,
        device_id=((z + (1 if way == 0 else RING - 1)) % RING, e),
        device_id_type=MESH,
    )
    copy.start()
    return copy


class RingSum:
    def __init__(self, stage, land, send, recv, half_width, z, e):
        self.stage, self.land, self.send, self.recv = stage, land, send, recv
        self.half_width, self.z, self.e, self.sent = half_width, z, e, {}

    def cols(self, half):
        return pl.ds(half * self.half_width, self.half_width)

    @staticmethod
    def block(way, step):
        return 4 - step if way == 0 else (4 + step) % RING

    def push(self, way, step, half):
        self.sent[way, step, half] = ring_send(
            self.stage.at[self.block(way, step), :, self.cols(half)],
            self.land.at[way, step, :, self.cols(half)],
            self.send.at[way, step, half],
            self.recv.at[way, step, half],
            way,
            self.z,
            self.e,
        )

    def add(self, way, step, half):
        self.sent[way, step - 1, half].wait_recv()
        k, part = self.block(way, step), self.cols(half)
        self.stage[k, :, part] = (
            self.stage[k, :, part].astype(F32) + self.land[way, step - 1, :, part].astype(F32)
        ).astype(BF16)
        self.push(way, step, half)

    def first(self):
        self.push(1, 0, 0)
        self.push(0, 0, 1)

    def free(self):
        self.push(0, 1, 0)
        self.push(1, 1, 1)

    def second(self):
        self.add(0, 1, 1)
        self.add(1, 1, 0)

    def later(self, step):
        for halves in ((0, 1), (1, 0)):
            for way in (0, 1):
                self.add(way, step, halves[way])

    def result(self, half):
        self.sent[0, 3, half].wait_recv()
        self.sent[1, 3, half].wait_recv()
        part = self.cols(half)
        return (
            self.stage[0, :, part].astype(F32)
            + self.land[0, 3, :, part].astype(F32)
            + self.land[1, 3, :, part].astype(F32)
        )

    def drain(self):
        for c in self.sent.values():
            c.wait_send()


def upright(row, n):
    same = lax.broadcasted_iota(jnp.int32, (n, n), 0) == lax.broadcasted_iota(jnp.int32, (n, n), 1)
    return jnp.sum(jnp.where(same, row, 0.0), axis=1, keepdims=True)


def attention_kernel(
    tokens, queries, memory, places, out_weight, gain, routes, shares,
    attended, normed, notes,
    weight, qbuf, kvbuf, posbuf, stage, land, total, own_tokens, own_gain,
    wsem, lsem, qs, qr, ks, kr, ps, pr, ns, nr, rs, rr,
):
    z, e = lax.axis_index("seq"), lax.axis_index("exp")
    barrier = pltpu.get_barrier_semaphore()
    peers = exp_peers(e)
    for k in range(1, RING):
        pl.semaphore_signal(barrier, inc=1, device_id=((z + k) % RING, e), device_id_type=MESH)
    for p in peers:
        pl.semaphore_signal(barrier, inc=1, device_id=(z, p), device_id_type=MESH)
    pair = pl.multiple_of(z // 2 * 256, 256)
    local = [
        pltpu.make_async_copy(queries.at[:, pl.ds(pl.multiple_of(z * KEYS, KEYS), KEYS)], qbuf.at[0], lsem.at[0]),
        pltpu.make_async_copy(memory.at[:, pl.ds(pair, 256)], kvbuf.at[31], lsem.at[1]),
        pltpu.make_async_copy(out_weight, weight, wsem),
        pltpu.make_async_copy(tokens, own_tokens, lsem.at[2]),
        pltpu.make_async_copy(gain, own_gain, lsem.at[3]),
    ]
    for c in local:
        c.start()
    posbuf[31] = jnp.broadcast_to(upright(places[...].astype(F32), 16), (16, 128))
    notes[0] = jnp.zeros((8, 128), F32)
    named = routes[...].astype(F32)
    notes[0, 0:2, :] = jnp.concatenate([named, named], axis=1)
    notes[0, 2:4, :] = jnp.concatenate([shares[...], shares[...]], axis=1)
    pl.semaphore_wait(barrier, RING - 1 + len(peers))
    queue, moved = {}, []
    for k in (4, 3, 5, 2, 6, 1, 7):
        to = (z + k) % RING
        queue[RING - k] = pltpu.make_async_remote_copy(
            src_ref=queries.at[:, pl.ds(pl.multiple_of(to * KEYS, KEYS), KEYS)],
            dst_ref=qbuf.at[RING - k],
            send_sem=qs.at[k],
            recv_sem=qr.at[RING - k],
            device_id=(to, e),
            device_id_type=MESH,
        )
        queue[RING - k].start()
    local[1].wait()
    for n, p in enumerate(peers):
        for src, dst, s, r in ((kvbuf.at[31], kvbuf, ks, kr), (posbuf.at[31], posbuf, ps, pr)):
            c = pltpu.make_async_remote_copy(
                src_ref=src, dst_ref=dst.at[n], send_sem=s.at[n], recv_sem=r.at[n],
                device_id=(z, p), device_id_type=MESH,
            )
            c.start()
            moved.append(c)
    noted = []
    for k in range(1, RING):
        c = pltpu.make_async_remote_copy(
            src_ref=notes.at[0], dst_ref=notes.at[RING - k], send_sem=ns.at[k], recv_sem=nr.at[RING - k],
            device_id=((z + k) % RING, e), device_id_type=MESH,
        )
        c.start()
        noted.append(c)
    local[0].wait()
    for c in moved:
        c.wait()
    local[2].wait()

    def compute(k):
        if k:
            queue[k].wait_recv()
        block = qbuf[k]
        stacked = jnp.concatenate([block[:, h * HD:(h + 1) * HD] for h in range(4)], axis=0)
        key_rows = kvbuf[:, :, 0:HD].reshape(MEM, HD)
        value_rows = kvbuf[:, :, HD:2 * HD].reshape(MEM, HD)
        scores = lax.dot_general(
            key_rows, stacked, (((1,), (1,)), ((), ())), preferred_element_type=F32
        ) * (1.0 / math.sqrt(HD))
        limit = MEM + (z + k) % RING * TOK + lax.broadcasted_iota(jnp.int32, (1, 4 * TOK), 1) % TOK
        where = posbuf[...].reshape(MEM, 128)
        where = jnp.concatenate([where, where], axis=1)
        scores = jnp.where(where <= limit.astype(F32), scores, -1e30)
        top = jnp.max(scores, axis=0, keepdims=True)
        weights = jnp.exp(scores - top)
        probs = (weights / jnp.sum(weights, axis=0, keepdims=True)).astype(BF16)
        context = lax.dot_general(
            probs, value_rows, (((0,), (0,)), ((), ())), preferred_element_type=F32
        ).astype(BF16)
        context = jnp.concatenate([context[h * TOK:(h + 1) * TOK] for h in range(4)], axis=1)

        @pl.loop(0, 4)
        def _(c):
            part = pl.ds(pl.multiple_of(c * 1024, 1024), 1024)
            stage[k, :, part] = jnp.dot(
                context, weight[:, part], preferred_element_type=F32
            ).astype(BF16)

    ring = RingSum(stage, land, rs, rr, D // 2, z, e)
    compute(4)
    ring.first()
    compute(3)
    compute(5)
    ring.free()
    ring.second()
    compute(2)
    compute(6)
    ring.later(2)
    compute(1)
    compute(7)
    ring.later(3)
    compute(0)
    local[3].wait()
    local[4].wait()
    square = jnp.zeros((TOK, 1), F32)
    for half in range(2):
        projected = ring.result(half)
        part = ring.cols(half)
        attended[:, part] = projected.astype(BF16)
        summed = own_tokens[:, part].astype(F32) + projected
        total[:, part] = summed
        square = square + jnp.sum(summed * summed, axis=1, keepdims=True)
    scale = lax.rsqrt(square * (1.0 / D) + 1e-6)
    for half in range(2):
        part = ring.cols(half)
        normed[:, part] = (total[:, part] * scale * own_gain[:, part]).astype(BF16)
    for c in noted:
        c.wait()
    for c in queue.values():
        c.wait_send()
    ring.drain()


def pack(rows, wide, out, blocks):
    for c in range(blocks):
        for r in range(CAP):
            wide[pl.ds(c * CAP + r, EXPERTS, stride=PIECE), :] = rows[
                r * EXPERTS:(r + 1) * EXPERTS, c * 128:(c + 1) * 128
            ]
    out[...] = wide[...].astype(BF16)


def unpack(got, wide, out, base, blocks):
    wide[...] = got[...].astype(F32)
    for c in range(blocks):
        for r in range(CAP):
            out[r * EXPERTS:(r + 1) * EXPERTS, base + c * 128:base + (c + 1) * 128] = wide[
                pl.ds(c * CAP + r, EXPERTS, stride=PIECE), :
            ].astype(BF16)


def expert_kernel(
    normed, notes, gate, up, down,
    mixture,
    gate_up, low, xs, stage, land, others, mixed, arrived, outgo, income, home,
    wide, returned, picks, mixers,
    wsem, own_sem, es, er, gs, gr, os_, or_, rs, rr, ms, mr,
):
    z, e = lax.axis_index("seq"), lax.axis_index("exp")
    loads = [
        pltpu.make_async_copy(gate, gate_up.at[0:UNITS], wsem.at[0]),
        pltpu.make_async_copy(up, gate_up.at[UNITS:2 * UNITS], wsem.at[1]),
        pltpu.make_async_copy(down, low, wsem.at[2]),
    ]
    for c in loads:
        c.start()
    barrier = pltpu.get_barrier_semaphore()
    peers = exp_peers(e)
    for k in (1, RING - 1):
        pl.semaphore_signal(barrier, inc=1, device_id=((z + k) % RING, e), device_id_type=MESH)
    for p in peers:
        pl.semaphore_signal(barrier, inc=1, device_id=(z, p), device_id_type=MESH)

    moves = {}

    def exchange(n, src, dst):
        mine = pl.ds(pl.multiple_of(e * PIECE, PIECE), PIECE)
        copies = []
        for i, p in enumerate(peers):
            c = pltpu.make_async_remote_copy(
                src_ref=src.at[pl.ds(pl.multiple_of(p * PIECE, PIECE), PIECE)],
                dst_ref=dst.at[mine],
                send_sem=es.at[n, i],
                recv_sem=er.at[n, i],
                device_id=(z, p),
                device_id_type=MESH,
            )
            c.start()
            copies.append(c)
        own = pltpu.make_async_copy(src.at[mine], dst.at[mine], own_sem.at[n])
        own.start()
        moves[n] = copies, own

    def landed(n):
        moves[n][1].wait()
        for c in moves[n][0]:
            c.wait_recv()

    def left(n):
        for c in moves[n][0]:
            c.wait_send()

    def route(k):
        note = notes[k]
        one, two = note[0:1], note[1:2]
        one_up, two_up = upright(one[:, 0:TOK], TOK), upright(two[:, 0:TOK], TOK)
        shape = (TOK, 128)
        before = lax.broadcasted_iota(jnp.int32, shape, 0) < lax.broadcasted_iota(jnp.int32, shape, 1) % TOK

        def count(hit):
            return jnp.sum(jnp.where(hit, 1.0, 0.0), axis=0, keepdims=True)

        slot_one = count((one_up == one) & before) * EXPERTS + one
        slot_two = (count(one_up == two) + count((two_up == two) & before)) * EXPERTS + two
        ids = lax.broadcasted_iota(jnp.int32, (SLOTS, 128), 0).astype(F32)
        first, second = ids == slot_one, ids == slot_two
        picks[k] = jnp.where(first | second, 1.0, 0.0)[:, 0:TOK].astype(BF16)
        share = jnp.where(first, note[2:3], 0.0) + jnp.where(second, note[3:4], 0.0)
        high = share.astype(BF16).astype(F32)
        lane = lax.broadcasted_iota(jnp.int32, (SLOTS, 128), 1)
        mixers[k] = jnp.where(lane < TOK, high, share - high).astype(BF16)

    def weighted(k, width):
        both = lax.dot_general(
            mixers[k], returned[:, 0:width], (((0,), (0,)), ((), ())), preferred_element_type=F32
        )
        return both[0:TOK] + both[TOK:2 * TOK]

    def choose(k, block):
        return jnp.dot(picks[k], block, preferred_element_type=F32)

    gone = {}

    def tell(way, step):
        k = (RING - step) % RING if way == 0 else step
        to = (k + RING - 1) % RING if way == 0 else k + 1
        part = pl.ds(0, WB) if step < 3 else pl.ds(way * HB2, HB2)
        source = others.at[k, :, part] if step else normed.at[:, pl.ds(WA, WB)]
        gone[way, step] = ring_send(
            source, others.at[to, :, part], os_.at[way, step], or_.at[way, step], way, z, e
        )

    def scatter(k):
        block = others[k] if k else normed[:, WA:D]
        pack(choose(k, block), wide, outgo.at[k], WB // 128)
        exchange(k, outgo.at[k], income.at[k])

    gathered = {}

    def pass_on(way, step, half):
        k = (RING - step) % RING if way == 0 else step
        to = (k + RING - 1) % RING if way == 0 else k + 1
        part = pl.ds(half * HA, HA)
        gathered[way, step, half] = ring_send(
            xs.at[k, :, part], xs.at[to, :, part], gs.at[way, step, half], gr.at[way, step, half], way, z, e
        )

    def compute(k):
        landed(k)
        unpack(income.at[k], wide, xs.at[k], WA, WB // 128)
        act = lax.dot_general(
            xs[k], gate_up[...], (((1,), (1,)), ((), ())), preferred_element_type=F32
        )
        gate_act, up_act = act[:, 0:UNITS], act[:, UNITS:2 * UNITS]
        hidden = (gate_act / (1.0 + jnp.exp(-gate_act)) * up_act).astype(BF16)

        @pl.loop(0, 4)
        def _(c):
            part = pl.ds(pl.multiple_of(c * 1024, 1024), 1024)
            stage[k, :, part] = jnp.dot(hidden, low[:, part], preferred_element_type=F32).astype(BF16)

    def give_back(k):
        pack(stage[k, :, WA:D].astype(F32), wide, income.at[k], WB // 128)
        exchange(10 + k, income.at[k], home.at[k])

    def mix(k):
        landed(10 + k)
        unpack(home.at[k], wide, returned, 0, WB // 128)
        mixed[k] = weighted(k, WB).astype(BF16)

    wide[...] = jnp.zeros_like(wide)
    route(0)
    pack(choose(0, normed[:, 0:HA]), wide, outgo.at[8], HA // 128)
    pl.semaphore_wait(barrier, 2 + len(peers))
    tell(0, 0)
    tell(1, 0)
    exchange(8, outgo.at[8], income.at[8])
    pack(choose(0, normed[:, HA:WA]), wide, outgo.at[9], HA // 128)
    exchange(9, outgo.at[9], income.at[9])
    scatter(0)
    for way in (0, 1):
        gone[way, 0].wait_recv()
        tell(way, 1)
    for k in (7, 1):
        route(k)
        scatter(k)
    for half in range(2):
        landed(8 + half)
        unpack(income.at[8 + half], wide, xs.at[0], half * HA, HA // 128)
        pass_on(0, 0, half)
        pass_on(1, 0, half)
    for way in (0, 1):
        gone[way, 1].wait_recv()
        tell(way, 2)
    for k in (6, 2):
        route(k)
        scatter(k)
    for way in (0, 1):
        gone[way, 2].wait_recv()
        tell(way, 3)
    for k in (5, 3):
        route(k)
        scatter(k)
    for way in (0, 1):
        gone[way, 3].wait_recv()
    route(4)
    scatter(4)
    for c in loads:
        c.wait()

    def forward(step):
        for half in range(2):
            for way in (0, 1):
                gathered[way, step - 1, half].wait_recv()
                pass_on(way, step, half)

    forward(1)
    compute(0)
    compute(7)
    compute(1)
    forward(2)
    compute(6)
    compute(2)
    gathered[0, 2, 0].wait_recv()
    pass_on(0, 3, 0)
    gathered[1, 2, 1].wait_recv()
    pass_on(1, 3, 1)
    gathered[0, 2, 1].wait_recv()
    gathered[1, 2, 0].wait_recv()
    compute(5)
    compute(3)
    ring = RingSum(stage, land, rs, rr, HA, z, e)
    ring.free()
    gathered[0, 3, 0].wait_recv()
    gathered[1, 3, 1].wait_recv()
    compute(4)
    ring.first()
    give_back(4)
    give_back(3)
    give_back(5)
    ring.second()
    give_back(2)
    give_back(6)
    ring.later(2)
    give_back(1)
    give_back(7)
    give_back(0)
    tail = RingSum(mixed, arrived, ms, mr, HB2, z, e)
    mix(4)
    tail.first()
    ring.later(3)
    mix(3)
    mix(5)
    tail.free()
    tail.second()
    for half in range(2):
        pack(ring.result(half), wide, income.at[8 + half], HA // 128)
        exchange(18 + half, income.at[8 + half], home.at[8 + half])
    mix(2)
    mix(6)
    tail.later(2)
    mix(1)
    mix(7)
    tail.later(3)
    mix(0)
    for half in range(2):
        landed(18 + half)
        unpack(home.at[8 + half], wide, returned, 0, HA // 128)
        mixture[:, half * HA:(half + 1) * HA] = weighted(0, HA).astype(BF16)
    for half in range(2):
        mixture[:, WA + half * HB2:WA + (half + 1) * HB2] = tail.result(half).astype(BF16)
    for n in range(20):
        left(n)
    for c in list(gone.values()) + list(gathered.values()):
        c.wait_send()
    ring.drain()
    tail.drain()


VM = pl.BlockSpec(memory_space=pltpu.VMEM)
HB = pl.BlockSpec(memory_space=pl.ANY)
DMA = pltpu.SemaphoreType.DMA


def body(tokens, queries, memory_kv, memory_pos, out_weight, norm_gain, routes, route_weights, gate_w, up_w, down_w):
    attended, normed, notes = pl.pallas_call(
        attention_kernel,
        name="attention",
        out_shape=[jax.ShapeDtypeStruct((TOK, D), BF16)] * 2 + [jax.ShapeDtypeStruct((RING, 8, 128), F32)],
        in_specs=[HB, HB, HB, VM, HB, HB, VM, VM],
        out_specs=[VM, VM, VM],
        scratch_shapes=[
            pltpu.VMEM((KEYS, D), BF16),
            pltpu.VMEM((RING, TOK, KEYS), BF16),
            pltpu.VMEM((32, 16, 256), BF16),
            pltpu.VMEM((32, 16, 128), F32),
            pltpu.VMEM((RING, TOK, D), BF16),
            pltpu.VMEM((2, 4, TOK, D), BF16),
            pltpu.VMEM((TOK, D), F32),
            pltpu.VMEM((TOK, D), BF16),
            pltpu.VMEM((1, D), F32),
            DMA, DMA((4,)), DMA((RING,)), DMA((RING,)),
            DMA((31,)), DMA((31,)), DMA((31,)), DMA((31,)), DMA((RING,)), DMA((RING,)),
            DMA((2, 4, 2)), DMA((2, 4, 2)),
        ],
        compiler_params=pltpu.CompilerParams(
            collective_id=0, has_side_effects=True, vmem_limit_bytes=40 * 2**20
        ),
    )(
        tokens.reshape(TOK, D), queries.reshape(TOK, D), memory_kv, memory_pos.reshape(1, 16), out_weight,
        norm_gain.reshape(1, D), jnp.swapaxes(routes[0], 0, 1), jnp.swapaxes(route_weights[0], 0, 1),
    )

    mixture = pl.pallas_call(
        expert_kernel,
        name="experts",
        out_shape=jax.ShapeDtypeStruct((TOK, D), BF16),
        in_specs=[VM, VM, HB, HB, HB],
        out_specs=VM,
        scratch_shapes=[
            pltpu.VMEM((2 * UNITS, D), BF16),
            pltpu.VMEM((UNITS, D), BF16),
            pltpu.VMEM((RING, SLOTS, D), BF16),
            pltpu.VMEM((RING, SLOTS, D), BF16),
            pltpu.VMEM((2, 4, SLOTS, WA), BF16),
            pltpu.VMEM((RING, TOK, WB), BF16),
            pltpu.VMEM((RING, TOK, WB), BF16),
            pltpu.VMEM((2, 4, TOK, WB), BF16),
            pltpu.VMEM((10, EXPERTS * PIECE, 128), BF16),
            pltpu.VMEM((10, EXPERTS * PIECE, 128), BF16),
            pltpu.VMEM((10, EXPERTS * PIECE, 128), BF16),
            pltpu.VMEM((EXPERTS * PIECE, 128), F32),
            pltpu.VMEM((SLOTS, WB), BF16),
            pltpu.VMEM((RING, SLOTS, TOK), BF16),
            pltpu.VMEM((RING, SLOTS, 128), BF16),
            DMA((3,)), DMA((20,)), DMA((20, 31)), DMA((20, 31)),
            DMA((2, 4, 2)), DMA((2, 4, 2)), DMA((2, 4)), DMA((2, 4)),
            DMA((2, 4, 2)), DMA((2, 4, 2)), DMA((2, 4, 2)), DMA((2, 4, 2)),
        ],
        compiler_params=pltpu.CompilerParams(
            collective_id=1, has_side_effects=True, vmem_limit_bytes=60 * 2**20
        ),
    )(
        normed, notes,
        jnp.swapaxes(gate_w[0], 0, 1), jnp.swapaxes(up_w[0], 0, 1), down_w[0],
    )
    return attended.reshape(1, TOK, D), mixture.reshape(1, TOK, D)


def solution(mesh):
    in_specs = (
        P("exp", "seq", None),
        P("exp", "seq", None),
        P("exp", None),
        P("exp"),
        P("seq", None),
        P(),
        P("exp", "seq", None),
        P("exp", "seq", None),
        P("exp", None, "seq"),
        P("exp", None, "seq"),
        P("exp", "seq", None),
    )
    out_specs = (P("exp", "seq", None), P("exp", "seq", None))
    return jax.shard_map(body, mesh=mesh, in_specs=in_specs, out_specs=out_specs, check_vma=False)
```

```python
import math

import jax
import jax.numpy as jnp
from jax import lax
from jax.experimental import pallas as pl
from jax.experimental.pallas import tpu as pltpu
from jax.sharding import PartitionSpec as P

MESH = pl.DeviceIdType.MESH
EXPERTS = 32
CAP = 5
RING = 8
D = 4096
WA = 2048
WB = D - WA
HA, HB2 = WA // 2, WB // 2
HD = 128
TOK = 64
MEM = 512
KEYS = 512
UNITS = 192
SLOTS = EXPERTS * CAP
PLACE = {0: 0, 7: 1, 1: 2, 6: 3, 2: 4, 5: 5, 3: 6, 4: 7}
F32 = jnp.float32
BF16 = jnp.bfloat16

HOPS = [
    (dx, dy, dc)
    for dc in range(2)
    for dx, dy in [
        (2, 2), (1, 1), (3, 3), (2, 1), (1, 2), (2, 3), (3, 2), (1, 3),
        (3, 1), (2, 0), (0, 2), (1, 0), (3, 0), (0, 1), (0, 3), (0, 0),
    ]
    if (dx, dy, dc) != (0, 0, 0)
]


def piece(blocks, group=1):
    return -(-blocks * CAP * group // 16) * 16


HOLD_A = EXPERTS * piece(HA // 128)
HOLD_B = EXPERTS * piece(WB // 128)
HOLD_PAIR = EXPERTS * piece(WB // 128, 2)


def exp_peers(e):
    x, y, c = e // 8, (e // 2) % 4, e % 2
    return [((x + dx) % 4 * 8) + ((y + dy) % 4 * 2) + (c + dc) % 2 for dx, dy, dc in HOPS]


def ring_send(src, dst, send, recv, way, z, e):
    copy = pltpu.make_async_remote_copy(
        src_ref=src,
        dst_ref=dst,
        send_sem=send,
        recv_sem=recv,
        device_id=((z + (1 if way == 0 else RING - 1)) % RING, e),
        device_id_type=MESH,
    )
    copy.start()
    return copy


class RingSum:
    def __init__(self, stage, land, send, recv, half_width, z, e):
        self.stage, self.land, self.send, self.recv = stage, land, send, recv
        self.half_width, self.z, self.e, self.sent = half_width, z, e, {}

    def cols(self, half):
        return pl.ds(half * self.half_width, self.half_width)

    @staticmethod
    def block(way, step):
        return 4 - step if way == 0 else (4 + step) % RING

    def push(self, way, step, half):
        self.sent[way, step, half] = ring_send(
            self.stage.at[PLACE[self.block(way, step)], :, self.cols(half)],
            self.land.at[way, step, :, self.cols(half)],
            self.send.at[way, step, half],
            self.recv.at[way, step, half],
            way,
            self.z,
            self.e,
        )

    def add(self, way, step, half):
        self.sent[way, step - 1, half].wait_recv()
        k, part = PLACE[self.block(way, step)], self.cols(half)
        self.stage[k, :, part] = (
            self.stage[k, :, part].astype(F32) + self.land[way, step - 1, :, part].astype(F32)
        ).astype(BF16)
        self.push(way, step, half)

    def first(self):
        self.push(1, 0, 0)
        self.push(0, 0, 1)

    def free(self):
        self.push(0, 1, 0)
        self.push(1, 1, 1)

    def second(self):
        self.add(0, 1, 1)
        self.add(1, 1, 0)

    def later(self, step):
        for halves in ((0, 1), (1, 0)):
            for way in (0, 1):
                self.add(way, step, halves[way])

    def result(self, half):
        self.sent[0, 3, half].wait_recv()
        self.sent[1, 3, half].wait_recv()
        part = self.cols(half)
        return (
            self.stage[0, :, part].astype(F32)
            + self.land[0, 3, :, part].astype(F32)
            + self.land[1, 3, :, part].astype(F32)
        )

    def drain(self):
        for c in self.sent.values():
            c.wait_send()


def upright(row, n):
    same = lax.broadcasted_iota(jnp.int32, (n, n), 0) == lax.broadcasted_iota(jnp.int32, (n, n), 1)
    return jnp.sum(jnp.where(same, row, 0.0), axis=1, keepdims=True)


def attention_kernel(
    tokens, queries, memory, places, out_weight, gain, routes, shares,
    attended, normed, notes,
    weight, qbuf, kvbuf, posbuf, stage, land, total, own_tokens, own_gain, own_places, own_routes, own_shares,
    wsem, lsem, qs, qr, ks, kr, ns, nr, rs, rr,
):
    z, e = lax.axis_index("seq"), lax.axis_index("exp")
    barrier = pltpu.get_barrier_semaphore()
    peers = exp_peers(e)
    for k in range(1, RING):
        pl.semaphore_signal(barrier, inc=1, device_id=((z + k) % RING, e), device_id_type=MESH)
    for p in peers:
        pl.semaphore_signal(barrier, inc=1, device_id=(z, p), device_id_type=MESH)
    pair = pl.multiple_of(z // 2 * 256, 256)
    local = [
        pltpu.make_async_copy(queries.at[:, pl.ds(pl.multiple_of(z * KEYS, KEYS), KEYS)], qbuf.at[0], lsem.at[0]),
        pltpu.make_async_copy(memory.at[:, pl.ds(pair, 256)], kvbuf.at[31, :, 0:256], lsem.at[1]),
        pltpu.make_async_copy(out_weight, weight, wsem),
        pltpu.make_async_copy(tokens, own_tokens, lsem.at[2]),
        pltpu.make_async_copy(gain, own_gain, lsem.at[3]),
        pltpu.make_async_copy(places, own_places, lsem.at[4]),
        pltpu.make_async_copy(routes, own_routes, lsem.at[5]),
        pltpu.make_async_copy(shares, own_shares, lsem.at[6]),
    ]
    for c in local:
        c.start()
    for c in local[5:8]:
        c.wait()
    upper = own_places[...] // 32
    kvbuf[31, :, 256:384] = jnp.where(
        lax.broadcasted_iota(jnp.int32, (16, 128), 1) < 64,
        upright(upper.astype(F32), 16),
        upright((own_places[...] - upper * 32).astype(F32), 16),
    ).astype(BF16)
    notes[0] = jnp.zeros((8, 128), F32)
    named = own_routes[...].astype(F32)
    notes[0, 0:2, :] = jnp.concatenate([named, named], axis=1)
    notes[0, 2:4, :] = jnp.concatenate([own_shares[...], own_shares[...]], axis=1)
    pl.semaphore_wait(barrier, RING - 1 + len(peers))
    queue = {}
    for k in (4, 3, 5, 2, 6, 1, 7):
        to = (z + k) % RING
        queue[RING - k] = pltpu.make_async_remote_copy(
            src_ref=queries.at[:, pl.ds(pl.multiple_of(to * KEYS, KEYS), KEYS)],
            dst_ref=qbuf.at[RING - k],
            send_sem=qs.at[k],
            recv_sem=qr.at[RING - k],
            device_id=(to, e),
            device_id_type=MESH,
        )
        queue[RING - k].start()
    local[1].wait()
    for n, p in enumerate(peers):
        pltpu.make_async_remote_copy(
            src_ref=kvbuf.at[31], dst_ref=kvbuf.at[n], send_sem=ks, recv_sem=kr,
            device_id=(z, p), device_id_type=MESH,
        ).start()
    moved = pltpu.make_async_remote_copy(
        src_ref=kvbuf.at[0:31], dst_ref=kvbuf.at[0:31], send_sem=ks, recv_sem=kr,
        device_id=(z, peers[0]), device_id_type=MESH,
    )
    noted = []
    for k in range(1, RING):
        c = pltpu.make_async_remote_copy(
            src_ref=notes.at[0], dst_ref=notes.at[RING - k], send_sem=ns.at[k], recv_sem=nr.at[RING - k],
            device_id=((z + k) % RING, e), device_id_type=MESH,
        )
        c.start()
        noted.append(c)
    local[0].wait()
    moved.wait_recv()
    both = kvbuf[:, :, 256:384].astype(F32).reshape(MEM, 128)
    posbuf[...] = jnp.broadcast_to(both[:, 0:1] * 32.0 + both[:, 64:65], (MEM, 128))
    local[2].wait()

    def compute(k):
        if k:
            queue[k].wait_recv()
        block = qbuf[k]
        stacked = jnp.concatenate([block[:, h * HD:(h + 1) * HD] for h in range(4)], axis=0)
        key_rows = kvbuf[:, :, 0:HD].reshape(MEM, HD)
        value_rows = kvbuf[:, :, HD:2 * HD].reshape(MEM, HD)
        scores = lax.dot_general(
            key_rows, stacked, (((1,), (1,)), ((), ())), preferred_element_type=F32
        ) * (1.0 / math.sqrt(HD))
        limit = MEM + (z + k) % RING * TOK + lax.broadcasted_iota(jnp.int32, (1, 4 * TOK), 1) % TOK
        where = jnp.concatenate([posbuf[...], posbuf[...]], axis=1)
        scores = jnp.where(where <= limit.astype(F32), scores, -1e30)
        top = jnp.max(scores, axis=0, keepdims=True)
        weights = jnp.exp(scores - top)
        probs = (weights / jnp.sum(weights, axis=0, keepdims=True)).astype(BF16)
        context = lax.dot_general(
            probs, value_rows, (((0,), (0,)), ((), ())), preferred_element_type=F32
        ).astype(BF16)
        context = jnp.concatenate([context[h * TOK:(h + 1) * TOK] for h in range(4)], axis=1)

        @pl.loop(0, 4)
        def _(c):
            part = pl.ds(pl.multiple_of(c * 1024, 1024), 1024)
            stage[PLACE[k], :, part] = jnp.dot(
                context, weight[:, part], preferred_element_type=F32
            ).astype(BF16)

    ring = RingSum(stage, land, rs, rr, D // 2, z, e)
    compute(4)
    ring.first()
    compute(3)
    compute(5)
    ring.free()
    ring.second()
    compute(2)
    compute(6)
    ring.later(2)
    compute(1)
    compute(7)
    ring.later(3)
    compute(0)
    local[3].wait()
    local[4].wait()
    square = jnp.zeros((TOK, 1), F32)
    for half in range(2):
        projected = ring.result(half)
        part = ring.cols(half)
        attended[:, part] = projected.astype(BF16)
        summed = own_tokens[:, part].astype(F32) + projected
        total[:, part] = summed
        square = square + jnp.sum(summed * summed, axis=1, keepdims=True)
    scale = lax.rsqrt(square * (1.0 / D) + 1e-6)
    for half in range(2):
        part = ring.cols(half)
        normed[:, part] = (total[:, part] * scale * own_gain[:, part]).astype(BF16)
    moved.wait_send()
    for c in noted:
        c.wait()
    for c in queue.values():
        c.wait_send()
    ring.drain()


def pack(parts, wide, out, blocks):
    size = piece(blocks, len(parts))
    for i, rows in enumerate(parts):
        for c in range(blocks):
            for r in range(CAP):
                wide[pl.ds((i * blocks + c) * CAP + r, EXPERTS, stride=size), :] = rows[
                    r * EXPERTS:(r + 1) * EXPERTS, c * 128:(c + 1) * 128
                ]
    out[...] = wide[0:EXPERTS * size].astype(BF16)


def unpack(got, wide, outs, base, blocks):
    size = piece(blocks, len(outs))
    wide[0:EXPERTS * size] = got[...].astype(F32)
    for i, out in enumerate(outs):
        for c in range(blocks):
            for r in range(CAP):
                out[r * EXPERTS:(r + 1) * EXPERTS, base + c * 128:base + (c + 1) * 128] = wide[
                    pl.ds((i * blocks + c) * CAP + r, EXPERTS, stride=size), :
                ].astype(BF16)


GROUPS = [(0,), (7, 1), (6, 2), (5, 3), (4,)]


def expert_kernel(
    normed, notes, gate, up, down,
    mixture,
    gate_up, low, xs, stage, land, others, mixed, arrived,
    outgo, income, home, outgo_a, income_a, home_a, outgo2, income2, home2,
    wide, returned, picks, mixers, own_normed, own_notes,
    wsem, own_sem, es, er, gs, gr, os_, or_, rs, rr, ms, mr,
):
    z, e = lax.axis_index("seq"), lax.axis_index("exp")
    barrier = pltpu.get_barrier_semaphore()
    peers = exp_peers(e)
    for k in (1, RING - 1):
        pl.semaphore_signal(barrier, inc=1, device_id=((z + k) % RING, e), device_id_type=MESH)
    for p in peers:
        pl.semaphore_signal(barrier, inc=1, device_id=(z, p), device_id_type=MESH)
    loads = [
        pltpu.make_async_copy(normed, own_normed, wsem.at[3]),
        pltpu.make_async_copy(notes, own_notes, wsem.at[4]),
        pltpu.make_async_copy(gate, gate_up.at[0:UNITS], wsem.at[0]),
        pltpu.make_async_copy(up, gate_up.at[UNITS:2 * UNITS], wsem.at[1]),
        pltpu.make_async_copy(down, low, wsem.at[2]),
    ]
    for c in loads:
        c.start()

    moves = {}

    def buffers(n):
        if n in (0, 4):
            return outgo.at[n // 4], income.at[n // 4], home.at[n // 4]
        if n in (5, 6):
            return outgo_a.at[n - 5], income_a.at[n - 5], home_a.at[n - 5]
        return outgo2.at[n - 1], income2.at[n - 1], home2.at[n - 1]

    def exchange(n, src, dst):
        size = src.shape[0] // EXPERTS
        mine = pl.ds(pl.multiple_of(e * size, 16), size)
        for p in peers:
            pltpu.make_async_remote_copy(
                src_ref=src.at[pl.ds(pl.multiple_of(p * size, 16), size)],
                dst_ref=dst.at[mine],
                send_sem=es.at[n],
                recv_sem=er.at[n],
                device_id=(z, p),
                device_id_type=MESH,
            ).start()
        own = pltpu.make_async_copy(src.at[mine], dst.at[mine], own_sem.at[n])
        own.start()
        rest = pl.ds(0, size * (EXPERTS - 1))
        moves[n] = own, pltpu.make_async_remote_copy(
            src_ref=src.at[rest], dst_ref=dst.at[rest], send_sem=es.at[n], recv_sem=er.at[n],
            device_id=(z, peers[0]), device_id_type=MESH,
        )

    def landed(n):
        moves[n][0].wait()
        moves[n][1].wait_recv()

    def route(k):
        note = own_notes[k]
        one, two = note[0:1], note[1:2]
        one_up, two_up = upright(one[:, 0:TOK], TOK), upright(two[:, 0:TOK], TOK)
        shape = (TOK, 128)
        before = lax.broadcasted_iota(jnp.int32, shape, 0) < lax.broadcasted_iota(jnp.int32, shape, 1) % TOK

        def count(hit):
            return jnp.sum(jnp.where(hit, 1.0, 0.0), axis=0, keepdims=True)

        slot_one = count((one_up == one) & before) * EXPERTS + one
        slot_two = (count(one_up == two) + count((two_up == two) & before)) * EXPERTS + two
        ids = lax.broadcasted_iota(jnp.int32, (SLOTS, 128), 0).astype(F32)
        first, second = ids == slot_one, ids == slot_two
        picks[k] = jnp.where(first | second, 1.0, 0.0)[:, 0:TOK].astype(BF16)
        share = jnp.where(first, note[2:3], 0.0) + jnp.where(second, note[3:4], 0.0)
        high = share.astype(BF16).astype(F32)
        lane = lax.broadcasted_iota(jnp.int32, (SLOTS, 128), 1)
        mixers[k] = jnp.where(lane < TOK, high, share - high).astype(BF16)

    def weighted(k, rows):
        both = lax.dot_general(
            mixers[k], rows, (((0,), (0,)), ((), ())), preferred_element_type=F32
        )
        return both[0:TOK] + both[TOK:2 * TOK]

    def choose(k, block):
        return jnp.dot(picks[k], block, preferred_element_type=F32)

    gone = {}

    def tell(way, step):
        k = (RING - step) % RING if way == 0 else step
        to = (k + RING - 1) % RING if way == 0 else k + 1
        part = pl.ds(0, WB) if step < 3 else pl.ds(way * HB2, HB2)
        source = others.at[k, :, part] if step else own_normed.at[:, pl.ds(WA, WB)]
        gone[way, step] = ring_send(
            source, others.at[to, :, part], os_.at[way, step], or_.at[way, step], way, z, e
        )

    def scatter(n):
        out, came, _ = buffers(n)
        pack(
            [choose(k, others[k] if k else own_normed[:, WA:D]) for k in GROUPS[n]], wide, out, WB // 128
        )
        exchange(n, out, came)

    gathered = {}

    def pass_on(way, step, half):
        k = (RING - step) % RING if way == 0 else step
        to = (k + RING - 1) % RING if way == 0 else k + 1
        part = pl.ds(half * HA, HA)
        gathered[way, step, half] = ring_send(
            xs.at[PLACE[k], :, part], xs.at[PLACE[to], :, part],
            gs.at[way, step, half], gr.at[way, step, half], way, z, e,
        )

    def compute(n):
        landed(n)
        group, start = len(GROUPS[n]), PLACE[GROUPS[n][0]]
        unpack(buffers(n)[1], wide, [xs.at[start + i] for i in range(group)], WA, WB // 128)
        rows = xs[start:start + group].reshape(group * SLOTS, D)
        act = lax.dot_general(
            rows, gate_up[...], (((1,), (1,)), ((), ())), preferred_element_type=F32
        )
        gate_act, up_act = act[:, 0:UNITS], act[:, UNITS:2 * UNITS]
        hidden = (gate_act / (1.0 + jnp.exp(-gate_act)) * up_act).astype(BF16)

        @pl.loop(0, 4)
        def _(c):
            part = pl.ds(pl.multiple_of(c * 1024, 1024), 1024)
            stage[start:start + group, :, part] = (
                jnp.dot(hidden, low[:, part], preferred_element_type=F32).astype(BF16)
            ).reshape(group, SLOTS, 1024)

    def give_back(n):
        _, came, back = buffers(n)
        pack([stage[PLACE[k], :, WA:D].astype(F32) for k in GROUPS[n]], wide, came, WB // 128)
        exchange(7 + n, came, back)

    def mix(n):
        landed(7 + n)
        group = GROUPS[n]
        unpack(buffers(n)[2], wide, [returned.at[i] for i in range(len(group))], 0, WB // 128)
        for i, k in enumerate(group):
            mixed[PLACE[k]] = weighted(k, returned[i, :, 0:WB]).astype(BF16)

    loads[1].wait()
    route(0)
    loads[0].wait()
    wide[...] = jnp.zeros_like(wide)
    pack([choose(0, own_normed[:, 0:HA])], wide, outgo_a.at[0], HA // 128)
    pl.semaphore_wait(barrier, 2 + len(peers))
    tell(0, 0)
    tell(1, 0)
    exchange(5, outgo_a.at[0], income_a.at[0])
    pack([choose(0, own_normed[:, HA:WA])], wide, outgo_a.at[1], HA // 128)
    exchange(6, outgo_a.at[1], income_a.at[1])
    for way in (0, 1):
        gone[way, 0].wait_recv()
        tell(way, 1)
    scatter(0)
    route(7)
    route(1)
    for way in (0, 1):
        gone[way, 1].wait_recv()
        tell(way, 2)
    for half in range(2):
        landed(5 + half)
        unpack(income_a.at[half], wide, [xs.at[0]], half * HA, HA // 128)
        pass_on(0, 0, half)
        pass_on(1, 0, half)
    for way in (0, 1):
        gone[way, 2].wait_recv()
        tell(way, 3)
    scatter(1)
    route(6)
    route(2)
    scatter(2)
    route(5)
    route(3)
    scatter(3)
    for way in (0, 1):
        gone[way, 3].wait_recv()
    route(4)
    scatter(4)
    for c in loads[2:]:
        c.wait()

    def forward(step):
        for half in range(2):
            for way in (0, 1):
                gathered[way, step - 1, half].wait_recv()
                pass_on(way, step, half)

    forward(1)
    compute(0)
    compute(1)
    forward(2)
    compute(2)
    gathered[0, 2, 0].wait_recv()
    pass_on(0, 3, 0)
    gathered[1, 2, 1].wait_recv()
    pass_on(1, 3, 1)
    gathered[0, 2, 1].wait_recv()
    gathered[1, 2, 0].wait_recv()
    compute(3)
    ring = RingSum(stage, land, rs, rr, HA, z, e)
    ring.free()
    gathered[0, 3, 0].wait_recv()
    gathered[1, 3, 1].wait_recv()
    compute(4)
    ring.first()
    give_back(4)
    give_back(3)
    ring.second()
    give_back(2)
    ring.later(2)
    give_back(1)
    give_back(0)
    tail = RingSum(mixed, arrived, ms, mr, HB2, z, e)
    mix(4)
    tail.first()
    ring.later(3)
    mix(3)
    tail.free()
    tail.second()
    for half in range(2):
        pack([ring.result(half)], wide, income_a.at[half], HA // 128)
        exchange(12 + half, income_a.at[half], home_a.at[half])
    mix(2)
    tail.later(2)
    mix(1)
    tail.later(3)
    mix(0)
    for half in range(2):
        landed(12 + half)
        unpack(home_a.at[half], wide, [returned.at[0]], 0, HA // 128)
        mixture[:, half * HA:(half + 1) * HA] = weighted(0, returned[0, :, 0:HA]).astype(BF16)
    for half in range(2):
        mixture[:, WA + half * HB2:WA + (half + 1) * HB2] = tail.result(half).astype(BF16)
    for n in range(14):
        moves[n][1].wait_send()
    for c in list(gone.values()) + list(gathered.values()):
        c.wait_send()
    ring.drain()
    tail.drain()


VM = pl.BlockSpec(memory_space=pltpu.VMEM)
HB = pl.BlockSpec(memory_space=pl.ANY)
DMA = pltpu.SemaphoreType.DMA


def body(tokens, queries, memory_kv, memory_pos, out_weight, norm_gain, routes, route_weights, gate_w, up_w, down_w):
    attended, normed, notes = pl.pallas_call(
        attention_kernel,
        name="attention",
        out_shape=[jax.ShapeDtypeStruct((TOK, D), BF16)] * 2 + [jax.ShapeDtypeStruct((RING, 8, 128), F32)],
        in_specs=[HB] * 8,
        out_specs=[VM, VM, VM],
        scratch_shapes=[
            pltpu.VMEM((KEYS, D), BF16),
            pltpu.VMEM((RING, TOK, KEYS), BF16),
            pltpu.VMEM((32, 16, 384), BF16),
            pltpu.VMEM((MEM, 128), F32),
            pltpu.VMEM((RING, TOK, D), BF16),
            pltpu.VMEM((2, 4, TOK, D), BF16),
            pltpu.VMEM((TOK, D), F32),
            pltpu.VMEM((TOK, D), BF16),
            pltpu.VMEM((1, D), F32),
            pltpu.VMEM((1, 16), jnp.int32),
            pltpu.VMEM((2, TOK), jnp.int32),
            pltpu.VMEM((2, TOK), F32),
            DMA, DMA((7,)), DMA((RING,)), DMA((RING,)),
            DMA, DMA, DMA((RING,)), DMA((RING,)),
            DMA((2, 4, 2)), DMA((2, 4, 2)),
        ],
        compiler_params=pltpu.CompilerParams(
            collective_id=0, has_side_effects=True, vmem_limit_bytes=60 * 2**20
        ),
    )(
        tokens.reshape(TOK, D), queries.reshape(TOK, D), memory_kv, memory_pos.reshape(1, 16), out_weight,
        norm_gain.reshape(1, D), jnp.swapaxes(routes[0], 0, 1), jnp.swapaxes(route_weights[0], 0, 1),
    )

    mixture = pl.pallas_call(
        expert_kernel,
        name="experts",
        out_shape=jax.ShapeDtypeStruct((TOK, D), BF16),
        in_specs=[HB] * 5,
        out_specs=VM,
        scratch_shapes=[
            pltpu.VMEM((2 * UNITS, D), BF16),
            pltpu.VMEM((UNITS, D), BF16),
            pltpu.VMEM((RING, SLOTS, D), BF16),
            pltpu.VMEM((RING, SLOTS, D), BF16),
            pltpu.VMEM((2, 4, SLOTS, WA), BF16),
            pltpu.VMEM((RING, TOK, WB), BF16),
            pltpu.VMEM((RING, TOK, WB), BF16),
            pltpu.VMEM((2, 4, TOK, WB), BF16),
            *[pltpu.VMEM((2, HOLD_B, 128), BF16)] * 3,
            *[pltpu.VMEM((2, HOLD_A, 128), BF16)] * 3,
            *[pltpu.VMEM((3, HOLD_PAIR, 128), BF16)] * 3,
            pltpu.VMEM((HOLD_PAIR, 128), F32),
            pltpu.VMEM((2, SLOTS, max(HA, WB)), BF16),
            pltpu.VMEM((RING, SLOTS, TOK), BF16),
            pltpu.VMEM((RING, SLOTS, 128), BF16),
            pltpu.VMEM((TOK, D), BF16),
            pltpu.VMEM((RING, 8, 128), F32),
            DMA((5,)), DMA((14,)), DMA((14,)), DMA((14,)),
            DMA((2, 4, 2)), DMA((2, 4, 2)), DMA((2, 4)), DMA((2, 4)),
            DMA((2, 4, 2)), DMA((2, 4, 2)), DMA((2, 4, 2)), DMA((2, 4, 2)),
        ],
        compiler_params=pltpu.CompilerParams(
            collective_id=1, has_side_effects=True, vmem_limit_bytes=60 * 2**20
        ),
    )(
        normed, notes,
        jnp.swapaxes(gate_w[0], 0, 1), jnp.swapaxes(up_w[0], 0, 1), down_w[0],
    )
    return attended.reshape(1, TOK, D), mixture.reshape(1, TOK, D)


def solution(mesh):
    in_specs = (
        P("exp", "seq", None),
        P("exp", "seq", None),
        P("exp", None),
        P("exp"),
        P("seq", None),
        P(),
        P("exp", "seq", None),
        P("exp", "seq", None),
        P("exp", None, "seq"),
        P("exp", None, "seq"),
        P("exp", "seq", None),
    )
    out_specs = (P("exp", "seq", None), P("exp", "seq", None))
    return jax.shard_map(body, mesh=mesh, in_specs=in_specs, out_specs=out_specs, check_vma=False)
```

```python
import math

import jax
import jax.numpy as jnp
from jax import lax
from jax.experimental import pallas as pl
from jax.experimental.pallas import tpu as pltpu
from jax.sharding import PartitionSpec as P

MESH = pl.DeviceIdType.MESH
EXPERTS = 32
CAP = 5
RING = 8
D = 4096
WA = 2048
WB = D - WA
HA, HB2 = WA // 2, WB // 2
HD = 128
TOK = 64
MEM = 512
KEYS = 512
UNITS = 192
SLOTS = EXPERTS * CAP
PLACE = {0: 0, 7: 1, 1: 2, 6: 3, 2: 4, 5: 5, 3: 6, 4: 7}
F32 = jnp.float32
BF16 = jnp.bfloat16

HOPS = [
    (dx, dy, dc)
    for dc in range(2)
    for dx, dy in [
        (2, 2), (1, 1), (3, 3), (2, 1), (1, 2), (2, 3), (3, 2), (1, 3),
        (3, 1), (2, 0), (0, 2), (1, 0), (3, 0), (0, 1), (0, 3), (0, 0),
    ]
    if (dx, dy, dc) != (0, 0, 0)
]


def piece(blocks, group=1):
    return -(-blocks * CAP * group // 16) * 16


HOLD_A = EXPERTS * piece(HA // 128)
HOLD_B = EXPERTS * piece(WB // 128)
HOLD_PAIR = EXPERTS * piece(WB // 128, 2)


def exp_peers(e):
    x, y, c = e // 8, (e // 2) % 4, e % 2
    return [((x + dx) % 4 * 8) + ((y + dy) % 4 * 2) + (c + dc) % 2 for dx, dy, dc in HOPS]


def ring_send(src, dst, send, recv, way, z, e):
    copy = pltpu.make_async_remote_copy(
        src_ref=src,
        dst_ref=dst,
        send_sem=send,
        recv_sem=recv,
        device_id=((z + (1 if way == 0 else RING - 1)) % RING, e),
        device_id_type=MESH,
    )
    copy.start()
    return copy


class RingSum:
    def __init__(self, terms, lands, send, recv, z, e):
        self.terms, self.lands, self.send, self.recv = terms, lands, send, recv
        self.z, self.e, self.sent = z, e, {}

    @staticmethod
    def block(way, step):
        return 4 - step if way == 0 else (4 + step) % RING

    def push(self, way, step, half):
        self.sent[way, step, half] = ring_send(
            self.terms(self.block(way, step), half),
            self.lands(way, step, half),
            self.send.at[way, step, half],
            self.recv.at[way, step, half],
            way,
            self.z,
            self.e,
        )

    def add(self, way, step, half):
        self.sent[way, step - 1, half].wait_recv()
        mine, came = self.terms(self.block(way, step), half), self.lands(way, step - 1, half)
        mine[...] = (mine[...].astype(F32) + came[...].astype(F32)).astype(BF16)
        self.push(way, step, half)

    def first(self):
        self.push(1, 0, 0)
        self.push(0, 0, 1)

    def free(self, way):
        self.push(way, 1, way)

    def second(self):
        self.add(0, 1, 1)
        self.add(1, 1, 0)

    def later(self, step):
        for halves in ((0, 1), (1, 0)):
            for way in (0, 1):
                self.add(way, step, halves[way])

    def arrive(self, half):
        self.sent[0, 3, half].wait_recv()
        self.sent[1, 3, half].wait_recv()

    def total(self, half):
        return (
            self.terms(0, half)[...].astype(F32)
            + self.lands(0, 3, half)[...].astype(F32)
            + self.lands(1, 3, half)[...].astype(F32)
        )

    def drain(self):
        for c in self.sent.values():
            c.wait_send()


def upright(row, n):
    same = lax.broadcasted_iota(jnp.int32, (n, n), 0) == lax.broadcasted_iota(jnp.int32, (n, n), 1)
    return jnp.sum(jnp.where(same, row, 0.0), axis=1, keepdims=True)


def pack(parts, wide, out, blocks):
    size = piece(blocks, len(parts))
    for i, rows in enumerate(parts):
        for c in range(blocks):
            for r in range(CAP):
                wide[pl.ds((i * blocks + c) * CAP + r, EXPERTS, stride=size), :] = rows[
                    r * EXPERTS:(r + 1) * EXPERTS, c * 128:(c + 1) * 128
                ]
    out[...] = wide[0:EXPERTS * size].astype(BF16)


def unpack(got, wide, outs, base, blocks):
    size = piece(blocks, len(outs))
    wide[0:EXPERTS * size] = got[...].astype(F32)
    for i, out in enumerate(outs):
        for c in range(blocks):
            for r in range(CAP):
                out[r * EXPERTS:(r + 1) * EXPERTS, base + c * 128:base + (c + 1) * 128] = wide[
                    pl.ds((i * blocks + c) * CAP + r, EXPERTS, stride=size), :
                ].astype(BF16)


GROUPS = [(0,), (7, 1), (6, 2), (5, 3), (4,)]


def layer_kernel(
    tokens, queries, memory, places, out_weight, gain, routes, shares, gate, up, down,
    attended, mixture,
    kvbuf, posbuf, own_gain, own_places, own_routes, own_shares,
    gate_up, low, xs, stage, land, others, mixed, arrived,
    outgo, income, home, outgo_a, income_a, home_a, outgo2, income2, home2,
    wide, returned, picks, mixers, own_normed, own_notes,
    lsem, qs, qr, ks, kr, ns, nr, ps, pr,
    wsem, own_sem, es, er, gs, gr, os_, or_, rs, rr, ms, mr,
):
    z, e = lax.axis_index("seq"), lax.axis_index("exp")
    barrier = pltpu.get_barrier_semaphore()
    peers = exp_peers(e)
    for k in range(1, RING):
        pl.semaphore_signal(barrier, inc=1, device_id=((z + k) % RING, e), device_id_type=MESH)
    for p in peers:
        pl.semaphore_signal(barrier, inc=1, device_id=(z, p), device_id_type=MESH)

    def asked(k):
        return arrived.at[k // 4, k % 4, :, 0:KEYS]

    pair = pl.multiple_of(z // 2 * 256, 256)
    local = [
        pltpu.make_async_copy(queries.at[:, pl.ds(pl.multiple_of(z * KEYS, KEYS), KEYS)], asked(0), lsem.at[0]),
        pltpu.make_async_copy(memory.at[:, pl.ds(pair, 256)], kvbuf.at[31, :, 0:256], lsem.at[1]),
        pltpu.make_async_copy(out_weight.at[0:128], xs.at[0, 0:128], wsem.at[3]),
        pltpu.make_async_copy(tokens.at[:, 0:WA], others.at[0], lsem.at[2]),
        pltpu.make_async_copy(gain, own_gain, lsem.at[3]),
        pltpu.make_async_copy(places, own_places, lsem.at[4]),
        pltpu.make_async_copy(routes, own_routes, lsem.at[5]),
        pltpu.make_async_copy(shares, own_shares, lsem.at[6]),
        pltpu.make_async_copy(tokens.at[:, WA:D], mixed.at[0], lsem.at[7]),
        pltpu.make_async_copy(out_weight.at[128:256], xs.at[1, 0:128], wsem.at[4]),
        pltpu.make_async_copy(out_weight.at[256:384], xs.at[2, 0:128], wsem.at[5]),
        pltpu.make_async_copy(out_weight.at[384:512], xs.at[3, 0:128], wsem.at[6]),
        pltpu.make_async_copy(gate, gate_up.at[0:UNITS], wsem.at[0]),
        pltpu.make_async_copy(up, gate_up.at[UNITS:2 * UNITS], wsem.at[1]),
        pltpu.make_async_copy(down, low, wsem.at[2]),
    ]
    for c in local:
        c.start()
    for c in local[5:8]:
        c.wait()
    upper = own_places[...] // 32
    kvbuf[31, :, 256:384] = jnp.where(
        lax.broadcasted_iota(jnp.int32, (16, 128), 1) < 64,
        upright(upper.astype(F32), 16),
        upright((own_places[...] - upper * 32).astype(F32), 16),
    ).astype(BF16)
    own_notes[0] = jnp.zeros((8, 128), F32)
    named = own_routes[...].astype(F32)
    own_notes[0, 0:2, :] = jnp.concatenate([named, named], axis=1)
    own_notes[0, 2:4, :] = jnp.concatenate([own_shares[...], own_shares[...]], axis=1)
    pl.semaphore_wait(barrier, RING - 1 + len(peers))
    queue = {}
    for k in (4, 3, 5, 2, 6, 1, 7):
        to = (z + k) % RING
        queue[RING - k] = pltpu.make_async_remote_copy(
            src_ref=queries.at[:, pl.ds(pl.multiple_of(to * KEYS, KEYS), KEYS)],
            dst_ref=asked(RING - k),
            send_sem=qs.at[k],
            recv_sem=qr.at[RING - k],
            device_id=(to, e),
            device_id_type=MESH,
        )
        queue[RING - k].start()
    local[1].wait()
    for n, p in enumerate(peers):
        pltpu.make_async_remote_copy(
            src_ref=kvbuf.at[31], dst_ref=kvbuf.at[n], send_sem=ks, recv_sem=kr,
            device_id=(z, p), device_id_type=MESH,
        ).start()
    moved = pltpu.make_async_remote_copy(
        src_ref=kvbuf.at[0:31], dst_ref=kvbuf.at[0:31], send_sem=ks, recv_sem=kr,
        device_id=(z, peers[0]), device_id_type=MESH,
    )
    noted = []
    for k in range(1, RING):
        c = pltpu.make_async_remote_copy(
            src_ref=own_notes.at[0], dst_ref=own_notes.at[RING - k], send_sem=ns.at[k], recv_sem=nr.at[RING - k],
            device_id=((z + k) % RING, e), device_id_type=MESH,
        )
        c.start()
        noted.append(c)
    local[0].wait()
    moved.wait_recv()
    both = kvbuf[:, :, 256:384].astype(F32).reshape(MEM, 128)
    posbuf[...] = jnp.broadcast_to(both[:, 0:1] * 32.0 + both[:, 64:65], (MEM, 128))
    for n in (2, 9, 10, 11):
        local[n].wait()

    def attend(k):
        if k:
            queue[k].wait_recv()
        block = asked(k)[...]
        stacked = jnp.concatenate([block[:, h * HD:(h + 1) * HD] for h in range(4)], axis=0)
        key_rows = kvbuf[:, :, 0:HD].reshape(MEM, HD)
        value_rows = kvbuf[:, :, HD:2 * HD].reshape(MEM, HD)
        scores = lax.dot_general(
            key_rows, stacked, (((1,), (1,)), ((), ())), preferred_element_type=F32
        ) * (1.0 / math.sqrt(HD))
        limit = MEM + (z + k) % RING * TOK + lax.broadcasted_iota(jnp.int32, (1, 4 * TOK), 1) % TOK
        where = jnp.concatenate([posbuf[...], posbuf[...]], axis=1)
        scores = jnp.where(where <= limit.astype(F32), scores, -1e30)
        top = jnp.max(scores, axis=0, keepdims=True)
        weights = jnp.exp(scores - top)
        probs = (weights / jnp.sum(weights, axis=0, keepdims=True)).astype(BF16)
        context = lax.dot_general(
            probs, value_rows, (((0,), (0,)), ((), ())), preferred_element_type=F32
        ).astype(BF16)
        context = jnp.concatenate([context[h * TOK:(h + 1) * TOK] for h in range(4)], axis=1)

        @pl.loop(0, 4)
        def _(c):
            part = pl.ds(pl.multiple_of(c * 1024, 1024), 1024)
            weight = xs[0:4, 0:128, part].reshape(KEYS, 1024)
            stage[PLACE[k], 0:TOK, part] = jnp.dot(
                context, weight, preferred_element_type=F32
            ).astype(BF16)

    moves = {}

    def buffers(n):
        if n in (0, 4):
            return outgo.at[n // 4], income.at[n // 4], home.at[n // 4]
        if n in (5, 6):
            return outgo_a.at[n - 5], income_a.at[n - 5], home_a.at[n - 5]
        return outgo2.at[n - 1], income2.at[n - 1], home2.at[n - 1]

    def exchange(n, src, dst):
        size = src.shape[0] // EXPERTS
        mine = pl.ds(pl.multiple_of(e * size, 16), size)
        for p in peers:
            pltpu.make_async_remote_copy(
                src_ref=src.at[pl.ds(pl.multiple_of(p * size, 16), size)],
                dst_ref=dst.at[mine],
                send_sem=es.at[n],
                recv_sem=er.at[n],
                device_id=(z, p),
                device_id_type=MESH,
            ).start()
        own = pltpu.make_async_copy(src.at[mine], dst.at[mine], own_sem.at[n])
        own.start()
        rest = pl.ds(0, size * (EXPERTS - 1))
        moves[n] = own, pltpu.make_async_remote_copy(
            src_ref=src.at[rest], dst_ref=dst.at[rest], send_sem=es.at[n], recv_sem=er.at[n],
            device_id=(z, peers[0]), device_id_type=MESH,
        )

    def landed(n):
        moves[n][0].wait()
        moves[n][1].wait_recv()

    def route(k):
        note = own_notes[k]
        one, two = note[0:1], note[1:2]
        one_up, two_up = upright(one[:, 0:TOK], TOK), upright(two[:, 0:TOK], TOK)
        shape = (TOK, 128)
        before = lax.broadcasted_iota(jnp.int32, shape, 0) < lax.broadcasted_iota(jnp.int32, shape, 1) % TOK

        def count(hit):
            return jnp.sum(jnp.where(hit, 1.0, 0.0), axis=0, keepdims=True)

        slot_one = count((one_up == one) & before) * EXPERTS + one
        slot_two = (count(one_up == two) + count((two_up == two) & before)) * EXPERTS + two
        ids = lax.broadcasted_iota(jnp.int32, (SLOTS, 128), 0).astype(F32)
        first, second = ids == slot_one, ids == slot_two
        picks[k] = jnp.where(first | second, 1.0, 0.0)[:, 0:TOK].astype(BF16)
        share = jnp.where(first, note[2:3], 0.0) + jnp.where(second, note[3:4], 0.0)
        high = share.astype(BF16).astype(F32)
        lane = lax.broadcasted_iota(jnp.int32, (SLOTS, 128), 1)
        mixers[k] = jnp.where(lane < TOK, high, share - high).astype(BF16)

    def weighted(k, rows):
        both = lax.dot_general(
            mixers[k], rows, (((0,), (0,)), ((), ())), preferred_element_type=F32
        )
        return both[0:TOK] + both[TOK:2 * TOK]

    def choose(k, block):
        return jnp.dot(picks[k], block, preferred_element_type=F32)

    gone = {}

    def tell(way, step):
        k = (RING - step) % RING if way == 0 else step
        to = (k + RING - 1) % RING if way == 0 else k + 1
        part = pl.ds(0, WB) if step < 3 else pl.ds(way * HB2, HB2)
        source = others.at[k, :, part] if step else own_normed.at[:, pl.ds(WA, WB)]
        gone[way, step] = ring_send(
            source, others.at[to, :, part], os_.at[way, step], or_.at[way, step], way, z, e
        )

    def scatter(n):
        out, came, _ = buffers(n)
        pack(
            [choose(k, others[k] if k else own_normed[:, WA:D]) for k in GROUPS[n]], wide, out, WB // 128
        )
        exchange(n, out, came)

    gathered = {}

    def pass_on(way, step, half):
        k = (RING - step) % RING if way == 0 else step
        to = (k + RING - 1) % RING if way == 0 else k + 1
        part = pl.ds(half * HA, HA)
        gathered[way, step, half] = ring_send(
            xs.at[PLACE[k], :, part], xs.at[PLACE[to], :, part],
            gs.at[way, step, half], gr.at[way, step, half], way, z, e,
        )

    def compute(n):
        landed(n)
        group, start = len(GROUPS[n]), PLACE[GROUPS[n][0]]
        unpack(buffers(n)[1], wide, [xs.at[start + i] for i in range(group)], WA, WB // 128)
        rows = xs[start:start + group].reshape(group * SLOTS, D)
        act = lax.dot_general(
            rows, gate_up[...], (((1,), (1,)), ((), ())), preferred_element_type=F32
        )
        gate_act, up_act = act[:, 0:UNITS], act[:, UNITS:2 * UNITS]
        hidden = (gate_act / (1.0 + jnp.exp(-gate_act)) * up_act).astype(BF16)

        @pl.loop(0, 4)
        def _(c):
            part = pl.ds(pl.multiple_of(c * 1024, 1024), 1024)
            stage[start:start + group, :, part] = (
                jnp.dot(hidden, low[:, part], preferred_element_type=F32).astype(BF16)
            ).reshape(group, SLOTS, 1024)

    def give_back(n):
        _, came, back = buffers(n)
        pack([stage[PLACE[k], :, WA:D].astype(F32) for k in GROUPS[n]], wide, came, WB // 128)
        exchange(7 + n, came, back)

    def mix(n):
        landed(7 + n)
        group = GROUPS[n]
        unpack(buffers(n)[2], wide, [returned.at[i] for i in range(len(group))], 0, WB // 128)
        for i, k in enumerate(group):
            mixed[PLACE[k]] = weighted(k, returned[i, :, 0:WB]).astype(BF16)

    front = RingSum(
        lambda k, half: stage.at[PLACE[k], 0:TOK, pl.ds(half * WA, WA)],
        lambda way, step, half: land.at[way, step, pl.ds(half * TOK, TOK), :],
        ps, pr, z, e,
    )
    attend(4)
    front.first()
    attend(3)
    front.free(0)
    attend(5)
    front.free(1)
    front.second()
    attend(2)
    attend(6)
    front.later(2)
    attend(1)
    attend(7)
    attend(0)
    front.later(3)
    for c in noted:
        c.wait()
    wide[...] = jnp.zeros_like(wide)
    for k in range(RING):
        route(k)
    for n in (3, 4, 8):
        local[n].wait()
    token_parts = others.at[0], mixed.at[0]
    square = jnp.zeros((TOK, 1), F32)
    for half in range(2):
        front.arrive(half)
        projected = front.total(half)
        stage[0, TOK:2 * TOK, half * WA:(half + 1) * WA] = projected.astype(BF16)
        summed = token_parts[half][...].astype(F32) + projected
        square = square + jnp.sum(summed * summed, axis=1, keepdims=True)
    result = pltpu.make_async_copy(stage.at[0, TOK:2 * TOK], attended, lsem.at[8])
    result.start()
    scale = lax.rsqrt(square * (1.0 / D) + 1e-6)

    def norm(half):
        part = pl.ds(half * WA, WA)
        summed = token_parts[half][...].astype(F32) + front.total(half)
        own_normed[:, part] = (summed * scale * own_gain[:, part]).astype(BF16)

    norm(1)
    tell(0, 0)
    tell(1, 0)
    norm(0)
    pack([choose(0, own_normed[:, 0:HA])], wide, outgo_a.at[0], HA // 128)
    exchange(5, outgo_a.at[0], income_a.at[0])
    pack([choose(0, own_normed[:, HA:WA])], wide, outgo_a.at[1], HA // 128)
    exchange(6, outgo_a.at[1], income_a.at[1])
    for way in (0, 1):
        gone[way, 0].wait_recv()
        tell(way, 1)
    scatter(0)
    for way in (0, 1):
        gone[way, 1].wait_recv()
        tell(way, 2)
    for half in range(2):
        landed(5 + half)
        unpack(income_a.at[half], wide, [xs.at[0]], half * HA, HA // 128)
        pass_on(0, 0, half)
        pass_on(1, 0, half)
    for way in (0, 1):
        gone[way, 2].wait_recv()
        tell(way, 3)
    scatter(1)
    scatter(2)
    scatter(3)
    for way in (0, 1):
        gone[way, 3].wait_recv()
    scatter(4)
    for n in (12, 13, 14):
        local[n].wait()
    front.drain()
    result.wait()

    def forward(step):
        for half in range(2):
            for way in (0, 1):
                gathered[way, step - 1, half].wait_recv()
                pass_on(way, step, half)

    forward(1)
    compute(0)
    compute(1)
    forward(2)
    compute(2)
    gathered[0, 2, 0].wait_recv()
    pass_on(0, 3, 0)
    gathered[1, 2, 1].wait_recv()
    pass_on(1, 3, 1)
    gathered[0, 2, 1].wait_recv()
    gathered[1, 2, 0].wait_recv()
    compute(3)
    ring = RingSum(
        lambda k, half: stage.at[PLACE[k], :, pl.ds(half * HA, HA)],
        lambda way, step, half: land.at[way, step, :, pl.ds(half * HA, HA)],
        rs, rr, z, e,
    )
    ring.free(0)
    ring.free(1)
    gathered[0, 3, 0].wait_recv()
    gathered[1, 3, 1].wait_recv()
    compute(4)
    ring.first()
    give_back(4)
    give_back(3)
    ring.second()
    give_back(2)
    ring.later(2)
    give_back(1)
    give_back(0)
    tail = RingSum(
        lambda k, half: mixed.at[PLACE[k], :, pl.ds(half * HB2, HB2)],
        lambda way, step, half: arrived.at[way, step, :, pl.ds(half * HB2, HB2)],
        ms, mr, z, e,
    )
    mix(4)
    tail.first()
    ring.later(3)
    mix(3)
    tail.free(0)
    tail.free(1)
    tail.second()
    for half in range(2):
        ring.arrive(half)
        pack([ring.total(half)], wide, income_a.at[half], HA // 128)
        exchange(12 + half, income_a.at[half], home_a.at[half])
    mix(2)
    tail.later(2)
    mix(1)
    tail.later(3)
    mix(0)
    for c in gone.values():
        c.wait_send()
    for half in range(2):
        landed(12 + half)
        unpack(home_a.at[half], wide, [returned.at[0]], 0, HA // 128)
        own_normed[:, half * HA:(half + 1) * HA] = weighted(0, returned[0, :, 0:HA]).astype(BF16)
    for half in range(2):
        tail.arrive(half)
        own_normed[:, WA + half * HB2:WA + (half + 1) * HB2] = tail.total(half).astype(BF16)
    result = pltpu.make_async_copy(own_normed, mixture, lsem.at[8])
    result.start()
    for n in range(14):
        moves[n][1].wait_send()
    for c in gathered.values():
        c.wait_send()
    result.wait()
    ring.drain()
    tail.drain()
    moved.wait_send()
    for c in queue.values():
        c.wait_send()


def settle_kernel(attended, mixture, attended_out, mixture_out, sem):
    copies = []
    for i, (src, dst) in enumerate(((attended, attended_out), (mixture, mixture_out))):
        for n in range(4):
            rows = pl.ds(16 * n, 16)
            copies.append(pltpu.make_async_copy(src.at[rows], dst.at[rows], sem.at[4 * i + n]))
    for c in copies:
        c.start()
    for c in copies:
        c.wait()


HB = pl.BlockSpec(memory_space=pl.ANY)
DMA = pltpu.SemaphoreType.DMA


def body(tokens, queries, memory_kv, memory_pos, out_weight, norm_gain, routes, route_weights, gate_w, up_w, down_w):
    attended, mixture = pl.pallas_call(
        layer_kernel,
        name="layer",
        out_shape=[jax.ShapeDtypeStruct((TOK, D), BF16)] * 2,
        in_specs=[HB] * 11,
        out_specs=[HB, HB],
        scratch_shapes=[
            pltpu.VMEM((32, 16, 384), BF16),
            pltpu.VMEM((MEM, 128), F32),
            pltpu.VMEM((1, D), F32),
            pltpu.VMEM((1, 16), jnp.int32),
            pltpu.VMEM((2, TOK), jnp.int32),
            pltpu.VMEM((2, TOK), F32),
            pltpu.VMEM((2 * UNITS, D), BF16),
            pltpu.VMEM((UNITS, D), BF16),
            pltpu.VMEM((RING, SLOTS, D), BF16),
            pltpu.VMEM((RING, SLOTS, D), BF16),
            pltpu.VMEM((2, 4, SLOTS, WA), BF16),
            pltpu.VMEM((RING, TOK, WB), BF16),
            pltpu.VMEM((RING, TOK, WB), BF16),
            pltpu.VMEM((2, 4, TOK, WB), BF16),
            *[pltpu.VMEM((2, HOLD_B, 128), BF16)] * 3,
            *[pltpu.VMEM((2, HOLD_A, 128), BF16)] * 3,
            *[pltpu.VMEM((3, HOLD_PAIR, 128), BF16)] * 3,
            pltpu.VMEM((HOLD_PAIR, 128), F32),
            pltpu.VMEM((2, SLOTS, max(HA, WB)), BF16),
            pltpu.VMEM((RING, SLOTS, TOK), BF16),
            pltpu.VMEM((RING, SLOTS, 128), BF16),
            pltpu.VMEM((TOK, D), BF16),
            pltpu.VMEM((RING, 8, 128), F32),
            DMA((9,)), DMA((RING,)), DMA((RING,)), DMA, DMA, DMA((RING,)), DMA((RING,)),
            DMA((2, 4, 2)), DMA((2, 4, 2)),
            DMA((7,)), DMA((14,)), DMA((14,)), DMA((14,)),
            DMA((2, 4, 2)), DMA((2, 4, 2)), DMA((2, 4)), DMA((2, 4)),
            DMA((2, 4, 2)), DMA((2, 4, 2)), DMA((2, 4, 2)), DMA((2, 4, 2)),
        ],
        compiler_params=pltpu.CompilerParams(
            collective_id=0, has_side_effects=True, vmem_limit_bytes=61 * 2**20
        ),
    )(
        tokens.reshape(TOK, D), queries.reshape(TOK, D), memory_kv, memory_pos.reshape(1, 16), out_weight,
        norm_gain.reshape(1, D), jnp.swapaxes(routes[0], 0, 1), jnp.swapaxes(route_weights[0], 0, 1),
        jnp.swapaxes(gate_w[0], 0, 1), jnp.swapaxes(up_w[0], 0, 1), down_w[0],
    )
    attended, mixture = pl.pallas_call(
        settle_kernel,
        name="settle",
        out_shape=[jax.ShapeDtypeStruct((TOK, D), BF16)] * 2,
        in_specs=[HB] * 2,
        out_specs=[HB] * 2,
        scratch_shapes=[DMA((8,))],
        compiler_params=pltpu.CompilerParams(vmem_limit_bytes=60 * 2**20),
    )(attended, mixture)
    return attended.reshape(1, TOK, D), mixture.reshape(1, TOK, D)


def solution(mesh):
    in_specs = (
        P("exp", "seq", None),
        P("exp", "seq", None),
        P("exp", None),
        P("exp"),
        P("seq", None),
        P(),
        P("exp", "seq", None),
        P("exp", "seq", None),
        P("exp", None, "seq"),
        P("exp", None, "seq"),
        P("exp", "seq", None),
    )
    out_specs = (P("exp", "seq", None), P("exp", "seq", None))
    return jax.shard_map(body, mesh=mesh, in_specs=in_specs, out_specs=out_specs, check_vma=False)
```

```python
import math

import jax
import jax.numpy as jnp
from jax import lax
from jax.experimental import pallas as pl
from jax.experimental.pallas import tpu as pltpu
from jax.sharding import PartitionSpec as P

MESH = pl.DeviceIdType.MESH
EXPERTS = 32
CAP = 5
RING = 8
D = 4096
WA = 2048
WB = D - WA
HA, HB2 = WA // 2, WB // 2
HD = 128
TOK = 64
MEM = 512
KEYS = 512
UNITS = 192
SLOTS = EXPERTS * CAP
PLACE = {0: 0, 7: 1, 1: 2, 6: 3, 2: 4, 5: 5, 3: 6, 4: 7}
F32 = jnp.float32
BF16 = jnp.bfloat16

HOPS = [
    (dx, dy, dc)
    for dc in range(2)
    for dx, dy in [
        (2, 2), (1, 1), (3, 3), (2, 1), (1, 2), (2, 3), (3, 2), (1, 3),
        (3, 1), (2, 0), (0, 2), (1, 0), (3, 0), (0, 1), (0, 3), (0, 0),
    ]
    if (dx, dy, dc) != (0, 0, 0)
]


def piece(blocks, group=1):
    return -(-blocks * CAP * group // 16) * 16


HOLD_A = EXPERTS * piece(HA // 128)
HOLD_B = EXPERTS * piece(WB // 128)
HOLD_PAIR = EXPERTS * piece(WB // 128, 2)


def exp_peers(e):
    x, y, c = e // 8, (e // 2) % 4, e % 2
    return [((x + dx) % 4 * 8) + ((y + dy) % 4 * 2) + (c + dc) % 2 for dx, dy, dc in HOPS]


def ring_send(src, dst, send, recv, way, z, e):
    copy = pltpu.make_async_remote_copy(
        src_ref=src,
        dst_ref=dst,
        send_sem=send,
        recv_sem=recv,
        device_id=((z + (1 if way == 0 else RING - 1)) % RING, e),
        device_id_type=MESH,
    )
    copy.start()
    return copy


class RingSum:
    def __init__(self, terms, lands, send, recv, z, e):
        self.terms, self.lands, self.send, self.recv = terms, lands, send, recv
        self.z, self.e, self.sent = z, e, {}

    @staticmethod
    def block(way, step):
        return 4 - step if way == 0 else (4 + step) % RING

    def push(self, way, step, half):
        self.sent[way, step, half] = ring_send(
            self.terms(self.block(way, step), half),
            self.lands(way, step, half),
            self.send.at[way, step, half],
            self.recv.at[way, step, half],
            way,
            self.z,
            self.e,
        )

    def add(self, way, step, half):
        self.sent[way, step - 1, half].wait_recv()
        mine, came = self.terms(self.block(way, step), half), self.lands(way, step - 1, half)
        mine[...] = (mine[...].astype(F32) + came[...].astype(F32)).astype(BF16)
        self.push(way, step, half)

    def first(self):
        self.push(1, 0, 0)
        self.push(0, 0, 1)

    def free(self, way):
        self.push(way, 1, way)

    def second(self):
        self.add(0, 1, 1)
        self.add(1, 1, 0)

    def later(self, step):
        for halves in ((0, 1), (1, 0)):
            for way in (0, 1):
                self.add(way, step, halves[way])

    def arrive(self, half):
        self.sent[0, 3, half].wait_recv()
        self.sent[1, 3, half].wait_recv()

    def total(self, half):
        return (
            self.terms(0, half)[...].astype(F32)
            + self.lands(0, 3, half)[...].astype(F32)
            + self.lands(1, 3, half)[...].astype(F32)
        )

    def drain(self):
        for c in self.sent.values():
            c.wait_send()


def upright(row, n):
    same = lax.broadcasted_iota(jnp.int32, (n, n), 0) == lax.broadcasted_iota(jnp.int32, (n, n), 1)
    return jnp.sum(jnp.where(same, row, 0.0), axis=1, keepdims=True)


def pack(parts, wide, out, blocks):
    size = piece(blocks, len(parts))
    for i, rows in enumerate(parts):
        for c in range(blocks):
            for r in range(CAP):
                wide[pl.ds((i * blocks + c) * CAP + r, EXPERTS, stride=size), :] = rows[
                    r * EXPERTS:(r + 1) * EXPERTS, c * 128:(c + 1) * 128
                ]
    out[...] = wide[0:EXPERTS * size].astype(BF16)


def unpack(got, wide, outs, base, blocks):
    size = piece(blocks, len(outs))
    wide[0:EXPERTS * size] = got[...].astype(F32)
    for i, out in enumerate(outs):
        for c in range(blocks):
            for r in range(CAP):
                out[r * EXPERTS:(r + 1) * EXPERTS, base + c * 128:base + (c + 1) * 128] = wide[
                    pl.ds((i * blocks + c) * CAP + r, EXPERTS, stride=size), :
                ].astype(BF16)


GROUPS = [(0,), (7, 1), (6, 2), (5, 3), (4,)]


def layer_kernel(
    tokens, queries, memory, places, out_weight, gain, routes, shares, gate, up, down,
    attended, mixture,
    kvbuf, posbuf, own_gain, own_places, own_routes, own_shares,
    gate_up, low, xs, stage, land, others, mixed, arrived,
    outgo, income, home, outgo_a, income_a, home_a, outgo2, income2, home2,
    wide, returned, picks, mixers, own_normed, own_notes,
    lsem, qs, qr, ks, kr, ns, nr, ps, pr,
    wsem, own_sem, es, er, gs, gr, os_, or_, rs, rr, ms, mr,
):
    z, e = lax.axis_index("seq"), lax.axis_index("exp")
    barrier = pltpu.get_barrier_semaphore()
    peers = exp_peers(e)
    for k in range(1, RING):
        pl.semaphore_signal(barrier, inc=1, device_id=((z + k) % RING, e), device_id_type=MESH)
    for p in peers:
        pl.semaphore_signal(barrier, inc=1, device_id=(z, p), device_id_type=MESH)

    def asked(k):
        return arrived.at[k // 4, k % 4, :, 0:KEYS]

    pair = pl.multiple_of(z // 2 * 256, 256)
    local = [
        pltpu.make_async_copy(queries.at[:, pl.ds(pl.multiple_of(z * KEYS, KEYS), KEYS)], asked(0), lsem.at[0]),
        pltpu.make_async_copy(memory.at[:, pl.ds(pair, 256)], kvbuf.at[31, :, 0:256], lsem.at[1]),
        pltpu.make_async_copy(out_weight.at[0:128], xs.at[0, 0:128], wsem.at[3]),
        pltpu.make_async_copy(tokens.at[:, 0:WA], others.at[0], lsem.at[2]),
        pltpu.make_async_copy(gain, own_gain, lsem.at[3]),
        pltpu.make_async_copy(places, own_places, lsem.at[4]),
        pltpu.make_async_copy(routes, own_routes, lsem.at[5]),
        pltpu.make_async_copy(shares, own_shares, lsem.at[6]),
        pltpu.make_async_copy(tokens.at[:, WA:D], mixed.at[0], lsem.at[7]),
        pltpu.make_async_copy(out_weight.at[128:256], xs.at[1, 0:128], wsem.at[4]),
        pltpu.make_async_copy(out_weight.at[256:384], xs.at[2, 0:128], wsem.at[5]),
        pltpu.make_async_copy(out_weight.at[384:512], xs.at[3, 0:128], wsem.at[6]),
        pltpu.make_async_copy(gate, gate_up.at[0:UNITS], wsem.at[0]),
        pltpu.make_async_copy(up, gate_up.at[UNITS:2 * UNITS], wsem.at[1]),
        pltpu.make_async_copy(down, low, wsem.at[2]),
    ]
    for c in local:
        c.start()
    for c in local[5:8]:
        c.wait()
    upper = own_places[...] // 32
    kvbuf[31, :, 256:384] = jnp.where(
        lax.broadcasted_iota(jnp.int32, (16, 128), 1) < 64,
        upright(upper.astype(F32), 16),
        upright((own_places[...] - upper * 32).astype(F32), 16),
    ).astype(BF16)
    own_notes[0] = jnp.zeros((8, 128), F32)
    named = own_routes[...].astype(F32)
    own_notes[0, 0:2, :] = jnp.concatenate([named, named], axis=1)
    own_notes[0, 2:4, :] = jnp.concatenate([own_shares[...], own_shares[...]], axis=1)
    pl.semaphore_wait(barrier, RING - 1 + len(peers))
    queue = {}
    for k in (4, 3, 5, 2, 6, 1, 7):
        to = (z + k) % RING
        queue[RING - k] = pltpu.make_async_remote_copy(
            src_ref=queries.at[:, pl.ds(pl.multiple_of(to * KEYS, KEYS), KEYS)],
            dst_ref=asked(RING - k),
            send_sem=qs.at[k],
            recv_sem=qr.at[RING - k],
            device_id=(to, e),
            device_id_type=MESH,
        )
        queue[RING - k].start()
    local[1].wait()
    for n, p in enumerate(peers):
        pltpu.make_async_remote_copy(
            src_ref=kvbuf.at[31], dst_ref=kvbuf.at[n], send_sem=ks, recv_sem=kr,
            device_id=(z, p), device_id_type=MESH,
        ).start()
    moved = pltpu.make_async_remote_copy(
        src_ref=kvbuf.at[0:31], dst_ref=kvbuf.at[0:31], send_sem=ks, recv_sem=kr,
        device_id=(z, peers[0]), device_id_type=MESH,
    )
    noted = []
    for k in range(1, RING):
        c = pltpu.make_async_remote_copy(
            src_ref=own_notes.at[0], dst_ref=own_notes.at[RING - k], send_sem=ns.at[k], recv_sem=nr.at[RING - k],
            device_id=((z + k) % RING, e), device_id_type=MESH,
        )
        c.start()
        noted.append(c)
    local[0].wait()
    moved.wait_recv()
    both = kvbuf[:, :, 256:384].astype(F32).reshape(MEM, 128)
    posbuf[...] = jnp.broadcast_to(both[:, 0:1] * 32.0 + both[:, 64:65], (MEM, 128))
    for n in (2, 9, 10, 11):
        local[n].wait()

    def attend(k):
        if k:
            queue[k].wait_recv()
        block = asked(k)[...]
        stacked = jnp.concatenate([block[:, h * HD:(h + 1) * HD] for h in range(4)], axis=0)
        key_rows = kvbuf[:, :, 0:HD].reshape(MEM, HD)
        value_rows = kvbuf[:, :, HD:2 * HD].reshape(MEM, HD)
        scores = lax.dot_general(
            key_rows, stacked, (((1,), (1,)), ((), ())), preferred_element_type=F32
        ) * (1.0 / math.sqrt(HD))
        limit = MEM + (z + k) % RING * TOK + lax.broadcasted_iota(jnp.int32, (1, 4 * TOK), 1) % TOK
        where = jnp.concatenate([posbuf[...], posbuf[...]], axis=1)
        scores = jnp.where(where <= limit.astype(F32), scores, -1e30)
        top = jnp.max(scores, axis=0, keepdims=True)
        weights = jnp.exp(scores - top)
        probs = (weights / jnp.sum(weights, axis=0, keepdims=True)).astype(BF16)
        context = lax.dot_general(
            probs, value_rows, (((0,), (0,)), ((), ())), preferred_element_type=F32
        ).astype(BF16)
        context = jnp.concatenate([context[h * TOK:(h + 1) * TOK] for h in range(4)], axis=1)

        @pl.loop(0, 4)
        def _(c):
            part = pl.ds(pl.multiple_of(c * 1024, 1024), 1024)
            weight = xs[0:4, 0:128, part].reshape(KEYS, 1024)
            stage[PLACE[k], 0:TOK, part] = jnp.dot(
                context, weight, preferred_element_type=F32
            ).astype(BF16)

    moves = {}

    def buffers(n):
        if n in (0, 4):
            return outgo.at[n // 4], income.at[n // 4], home.at[n // 4]
        if n in (5, 6):
            return outgo_a.at[n - 5], income_a.at[n - 5], home_a.at[n - 5]
        return outgo2.at[n - 1], income2.at[n - 1], home2.at[n - 1]

    def exchange(n, src, dst):
        size = src.shape[0] // EXPERTS
        mine = pl.ds(pl.multiple_of(e * size, 16), size)
        for p in peers:
            pltpu.make_async_remote_copy(
                src_ref=src.at[pl.ds(pl.multiple_of(p * size, 16), size)],
                dst_ref=dst.at[mine],
                send_sem=es.at[n],
                recv_sem=er.at[n],
                device_id=(z, p),
                device_id_type=MESH,
            ).start()
        own = pltpu.make_async_copy(src.at[mine], dst.at[mine], own_sem.at[n])
        own.start()
        rest = pl.ds(0, size * (EXPERTS - 1))
        moves[n] = own, pltpu.make_async_remote_copy(
            src_ref=src.at[rest], dst_ref=dst.at[rest], send_sem=es.at[n], recv_sem=er.at[n],
            device_id=(z, peers[0]), device_id_type=MESH,
        )

    def landed(n):
        moves[n][0].wait()
        moves[n][1].wait_recv()

    def route(k):
        note = own_notes[k]
        one, two = note[0:1], note[1:2]
        one_up, two_up = upright(one[:, 0:TOK], TOK), upright(two[:, 0:TOK], TOK)
        shape = (TOK, 128)
        before = lax.broadcasted_iota(jnp.int32, shape, 0) < lax.broadcasted_iota(jnp.int32, shape, 1) % TOK

        def count(hit):
            return jnp.sum(jnp.where(hit, 1.0, 0.0), axis=0, keepdims=True)

        slot_one = count((one_up == one) & before) * EXPERTS + one
        slot_two = (count(one_up == two) + count((two_up == two) & before)) * EXPERTS + two
        ids = lax.broadcasted_iota(jnp.int32, (SLOTS, 128), 0).astype(F32)
        first, second = ids == slot_one, ids == slot_two
        picks[k] = jnp.where(first | second, 1.0, 0.0)[:, 0:TOK].astype(BF16)
        share = jnp.where(first, note[2:3], 0.0) + jnp.where(second, note[3:4], 0.0)
        high = share.astype(BF16).astype(F32)
        lane = lax.broadcasted_iota(jnp.int32, (SLOTS, 128), 1)
        mixers[k] = jnp.where(lane < TOK, high, share - high).astype(BF16)

    def weighted(k, rows):
        both = lax.dot_general(
            mixers[k], rows, (((0,), (0,)), ((), ())), preferred_element_type=F32
        )
        return both[0:TOK] + both[TOK:2 * TOK]

    def choose(k, block):
        return jnp.dot(picks[k], block, preferred_element_type=F32)

    gone = {}

    def tell(way, step):
        k = (RING - step) % RING if way == 0 else step
        to = (k + RING - 1) % RING if way == 0 else k + 1
        part = pl.ds(0, WB) if step < 3 else pl.ds(way * HB2, HB2)
        source = others.at[k, :, part] if step else own_normed.at[:, pl.ds(WA, WB)]
        gone[way, step] = ring_send(
            source, others.at[to, :, part], os_.at[way, step], or_.at[way, step], way, z, e
        )

    def scatter(n):
        out, came, _ = buffers(n)
        pack(
            [choose(k, others[k] if k else own_normed[:, WA:D]) for k in GROUPS[n]], wide, out, WB // 128
        )
        exchange(n, out, came)

    gathered = {}

    def pass_on(way, step, half):
        k = (RING - step) % RING if way == 0 else step
        to = (k + RING - 1) % RING if way == 0 else k + 1
        part = pl.ds(half * HA, HA)
        gathered[way, step, half] = ring_send(
            xs.at[PLACE[k], :, part], xs.at[PLACE[to], :, part],
            gs.at[way, step, half], gr.at[way, step, half], way, z, e,
        )

    def compute(n):
        landed(n)
        group, start = len(GROUPS[n]), PLACE[GROUPS[n][0]]
        unpack(buffers(n)[1], wide, [xs.at[start + i] for i in range(group)], WA, WB // 128)
        rows = xs[start:start + group].reshape(group * SLOTS, D)
        act = lax.dot_general(
            rows, gate_up[...], (((1,), (1,)), ((), ())), preferred_element_type=F32
        )
        gate_act, up_act = act[:, 0:UNITS], act[:, UNITS:2 * UNITS]
        hidden = (gate_act / (1.0 + jnp.exp(-gate_act)) * up_act).astype(BF16)

        @pl.loop(0, 4)
        def _(c):
            part = pl.ds(pl.multiple_of(c * 1024, 1024), 1024)
            stage[start:start + group, :, part] = (
                jnp.dot(hidden, low[:, part], preferred_element_type=F32).astype(BF16)
            ).reshape(group, SLOTS, 1024)

    def give_back(n):
        _, came, back = buffers(n)
        pack([stage[PLACE[k], :, WA:D].astype(F32) for k in GROUPS[n]], wide, came, WB // 128)
        exchange(7 + n, came, back)

    def mix(n):
        landed(7 + n)
        group = GROUPS[n]
        unpack(buffers(n)[2], wide, [returned.at[i] for i in range(len(group))], 0, WB // 128)
        for i, k in enumerate(group):
            mixed[PLACE[k]] = weighted(k, returned[i, :, 0:WB]).astype(BF16)

    front = RingSum(
        lambda k, half: stage.at[PLACE[k], 0:TOK, pl.ds(half * WA, WA)],
        lambda way, step, half: land.at[way, step, pl.ds(half * TOK, TOK), :],
        ps, pr, z, e,
    )
    attend(4)
    front.first()
    attend(3)
    front.free(0)
    attend(5)
    front.free(1)
    front.second()
    attend(2)
    attend(6)
    front.later(2)
    attend(1)
    attend(7)
    attend(0)
    front.later(3)
    for c in noted:
        c.wait()
    wide[...] = jnp.zeros_like(wide)
    for k in range(RING):
        route(k)
    for n in (3, 4, 8):
        local[n].wait()
    token_parts = others.at[0], mixed.at[0]
    square = jnp.zeros((TOK, 1), F32)
    for half in range(2):
        front.arrive(half)
        projected = front.total(half)
        stage[0, TOK:2 * TOK, half * WA:(half + 1) * WA] = projected.astype(BF16)
        summed = token_parts[half][...].astype(F32) + projected
        square = square + jnp.sum(summed * summed, axis=1, keepdims=True)
    result = pltpu.make_async_copy(stage.at[0, TOK:2 * TOK], attended, lsem.at[8])
    result.start()
    scale = lax.rsqrt(square * (1.0 / D) + 1e-6)

    def norm(half):
        part = pl.ds(half * WA, WA)
        summed = token_parts[half][...].astype(F32) + front.total(half)
        own_normed[:, part] = (summed * scale * own_gain[:, part]).astype(BF16)

    norm(1)
    tell(0, 0)
    tell(1, 0)
    norm(0)
    pack([choose(0, own_normed[:, 0:HA])], wide, outgo_a.at[0], HA // 128)
    exchange(5, outgo_a.at[0], income_a.at[0])
    pack([choose(0, own_normed[:, HA:WA])], wide, outgo_a.at[1], HA // 128)
    exchange(6, outgo_a.at[1], income_a.at[1])
    for way in (0, 1):
        gone[way, 0].wait_recv()
        tell(way, 1)
    scatter(0)
    for way in (0, 1):
        gone[way, 1].wait_recv()
        tell(way, 2)
    for half in range(2):
        landed(5 + half)
        unpack(income_a.at[half], wide, [xs.at[0]], half * HA, HA // 128)
        pass_on(0, 0, half)
        pass_on(1, 0, half)
    for way in (0, 1):
        gone[way, 2].wait_recv()
        tell(way, 3)
    scatter(1)
    scatter(2)
    scatter(3)
    for way in (0, 1):
        gone[way, 3].wait_recv()
    scatter(4)
    for n in (12, 13, 14):
        local[n].wait()
    front.drain()
    result.wait()

    def forward(step):
        for half in range(2):
            for way in (0, 1):
                gathered[way, step - 1, half].wait_recv()
                pass_on(way, step, half)

    forward(1)
    compute(0)
    compute(1)
    forward(2)
    compute(2)
    gathered[0, 2, 0].wait_recv()
    pass_on(0, 3, 0)
    gathered[1, 2, 1].wait_recv()
    pass_on(1, 3, 1)
    gathered[0, 2, 1].wait_recv()
    gathered[1, 2, 0].wait_recv()
    compute(3)
    ring = RingSum(
        lambda k, half: stage.at[PLACE[k], :, pl.ds(half * HA, HA)],
        lambda way, step, half: land.at[way, step, :, pl.ds(half * HA, HA)],
        rs, rr, z, e,
    )
    ring.free(0)
    ring.free(1)
    gathered[0, 3, 0].wait_recv()
    gathered[1, 3, 1].wait_recv()
    compute(4)
    ring.first()
    give_back(4)
    give_back(3)
    ring.second()
    give_back(2)
    ring.later(2)
    give_back(1)
    give_back(0)
    tail = RingSum(
        lambda k, half: mixed.at[PLACE[k], :, pl.ds(half * HB2, HB2)],
        lambda way, step, half: arrived.at[way, step, :, pl.ds(half * HB2, HB2)],
        ms, mr, z, e,
    )
    mix(4)
    tail.first()
    ring.later(3)
    mix(3)
    tail.free(0)
    tail.free(1)
    tail.second()
    for half in range(2):
        ring.arrive(half)
        pack([ring.total(half)], wide, income_a.at[half], HA // 128)
        exchange(12 + half, income_a.at[half], home_a.at[half])
    mix(2)
    tail.later(2)
    mix(1)
    tail.later(3)
    mix(0)
    for c in gone.values():
        c.wait_send()
    for half in range(2):
        landed(12 + half)
        unpack(home_a.at[half], wide, [returned.at[0]], 0, HA // 128)
        own_normed[:, half * HA:(half + 1) * HA] = weighted(0, returned[0, :, 0:HA]).astype(BF16)
    for half in range(2):
        tail.arrive(half)
        own_normed[:, WA + half * HB2:WA + (half + 1) * HB2] = tail.total(half).astype(BF16)
    result = pltpu.make_async_copy(own_normed, mixture, lsem.at[8])
    result.start()
    for n in range(14):
        moves[n][1].wait_send()
    for c in gathered.values():
        c.wait_send()
    result.wait()
    ring.drain()
    tail.drain()
    moved.wait_send()
    for c in queue.values():
        c.wait_send()


def settle_kernel(attended, mixture, attended_out, mixture_out, held, came, went):
    loads, stores = [], []
    for i, (src, dst) in enumerate(((attended, attended_out), (mixture, mixture_out))):
        for n in range(4):
            rows = pl.ds(16 * n, 16)
            loads.append(pltpu.make_async_copy(src.at[rows], held.at[i, rows], came.at[4 * i + n]))
            stores.append(pltpu.make_async_copy(held.at[i, rows], dst.at[rows], went.at[4 * i + n]))
    for c in loads:
        c.start()
    for c, d in zip(loads, stores):
        c.wait()
        d.start()
    for d in stores:
        d.wait()


HB = pl.BlockSpec(memory_space=pl.ANY)
DMA = pltpu.SemaphoreType.DMA


def body(tokens, queries, memory_kv, memory_pos, out_weight, norm_gain, routes, route_weights, gate_w, up_w, down_w):
    attended, mixture = pl.pallas_call(
        layer_kernel,
        name="layer",
        out_shape=[jax.ShapeDtypeStruct((TOK, D), BF16)] * 2,
        in_specs=[HB] * 11,
        out_specs=[HB, HB],
        scratch_shapes=[
            pltpu.VMEM((32, 16, 384), BF16),
            pltpu.VMEM((MEM, 128), F32),
            pltpu.VMEM((1, D), F32),
            pltpu.VMEM((1, 16), jnp.int32),
            pltpu.VMEM((2, TOK), jnp.int32),
            pltpu.VMEM((2, TOK), F32),
            pltpu.VMEM((2 * UNITS, D), BF16),
            pltpu.VMEM((UNITS, D), BF16),
            pltpu.VMEM((RING, SLOTS, D), BF16),
            pltpu.VMEM((RING, SLOTS, D), BF16),
            pltpu.VMEM((2, 4, SLOTS, WA), BF16),
            pltpu.VMEM((RING, TOK, WB), BF16),
            pltpu.VMEM((RING, TOK, WB), BF16),
            pltpu.VMEM((2, 4, TOK, WB), BF16),
            *[pltpu.VMEM((2, HOLD_B, 128), BF16)] * 3,
            *[pltpu.VMEM((2, HOLD_A, 128), BF16)] * 3,
            *[pltpu.VMEM((3, HOLD_PAIR, 128), BF16)] * 3,
            pltpu.VMEM((HOLD_PAIR, 128), F32),
            pltpu.VMEM((2, SLOTS, max(HA, WB)), BF16),
            pltpu.VMEM((RING, SLOTS, TOK), BF16),
            pltpu.VMEM((RING, SLOTS, 128), BF16),
            pltpu.VMEM((TOK, D), BF16),
            pltpu.VMEM((RING, 8, 128), F32),
            DMA((9,)), DMA((RING,)), DMA((RING,)), DMA, DMA, DMA((RING,)), DMA((RING,)),
            DMA((2, 4, 2)), DMA((2, 4, 2)),
            DMA((7,)), DMA((14,)), DMA((14,)), DMA((14,)),
            DMA((2, 4, 2)), DMA((2, 4, 2)), DMA((2, 4)), DMA((2, 4)),
            DMA((2, 4, 2)), DMA((2, 4, 2)), DMA((2, 4, 2)), DMA((2, 4, 2)),
        ],
        compiler_params=pltpu.CompilerParams(
            collective_id=0, has_side_effects=True, vmem_limit_bytes=61 * 2**20
        ),
    )(
        tokens.reshape(TOK, D), queries.reshape(TOK, D), memory_kv, memory_pos.reshape(1, 16), out_weight,
        norm_gain.reshape(1, D), jnp.swapaxes(routes[0], 0, 1), jnp.swapaxes(route_weights[0], 0, 1),
        jnp.swapaxes(gate_w[0], 0, 1), jnp.swapaxes(up_w[0], 0, 1), down_w[0],
    )
    attended, mixture = pl.pallas_call(
        settle_kernel,
        name="settle",
        out_shape=[jax.ShapeDtypeStruct((TOK, D), BF16)] * 2,
        in_specs=[HB] * 2,
        out_specs=[HB] * 2,
        scratch_shapes=[pltpu.VMEM((2, TOK, D), BF16), DMA((8,)), DMA((8,))],
        compiler_params=pltpu.CompilerParams(vmem_limit_bytes=60 * 2**20),
    )(attended, mixture)
    return attended.reshape(1, TOK, D), mixture.reshape(1, TOK, D)


def solution(mesh):
    in_specs = (
        P("exp", "seq", None),
        P("exp", "seq", None),
        P("exp", None),
        P("exp"),
        P("seq", None),
        P(),
        P("exp", "seq", None),
        P("exp", "seq", None),
        P("exp", None, "seq"),
        P("exp", None, "seq"),
        P("exp", "seq", None),
    )
    out_specs = (P("exp", "seq", None), P("exp", "seq", None))
    return jax.shard_map(body, mesh=mesh, in_specs=in_specs, out_specs=out_specs, check_vma=False)
```
